256 devices in a mesh: seq: 32 (over z, y_lo, core), section: 8 (over y_hi, x).
Axes of the slice: x: 4, y: 4 (y_hi: 2, y_lo: 2; y = y_hi * 2 + y_lo), z: 8, core: 2. Of those that a mesh axis runs over, the one named last changes fastest.
Arguments:
- inputs: bfloat16 [8, 4096, 2048], P('section', 'seq'), may hold values from -6 to 6
- b_proj: bfloat16 [8, 4096, 128], P('section', 'seq'), may hold values from -0.59765625 to 0.59765625
- c_proj: bfloat16 [8, 4096, 128], P('section', 'seq'), may hold values from -0.59765625 to 0.59765625
- decay_log: float32 [8, 4096, 32], P('section', 'seq'), may hold values from -1 to 0, as said below
- level_weight: float32 [8, 4096, 6, 32], P('section', 'seq'), may hold values from 0.25 to 2
- out_grad: bfloat16 [8, 4096, 2048], P('section', 'seq'), may hold values from -6 to 6
- final_state_grad: float32 [8, 32, 128, 64], P('section'), may hold values from -0.125 to 0.125
Outputs:
- upstream_grad: bfloat16 [8, 4096, 2048], P('section', 'seq')
- b_grad: float32 [8, 4096, 128], P('section', 'seq')
- c_grad: float32 [8, 4096, 128], P('section', 'seq')
- decay_grad: float32 [8, 4096, 32], P('section', 'seq')
- weight_grad: float32 [8, 4096, 6, 32], P('section', 'seq')
The draws below stay inside these ranges and needn't reach their ends.
Inputs may be any that keep to these rules, and one draw needn't show every extreme that they name: `decay_log`: negative; per head a rate that varies from token to token and from block to block.
All inputs are finite; a program needn't handle non-finite values.
Results may differ from the reference program's by a relative error of at most 0.001.
Values may be sent and summed in bfloat16 or wider, within the bound.
A program may use at most 128 MiB of HBM per device.

```python
import math
import jax
import jax.numpy as jnp
from jax import lax

HEAD_TOTAL = 32
P_SIZE = 64
N = 128
TOK_DEV = 128
BITS = 5
LEVELS = 6
SEQUENCE_TOKENS = 4096
RELAY_SECTIONS = 8
N_SEQ = 32


def draw_decay_log(key, part):
    random_keys = jax.random.split(key, 6)
    slow_share = 0.5
    slow_heads = jax.random.uniform(random_keys[0], (RELAY_SECTIONS, 1, HEAD_TOTAL)) < slow_share
    fast_rate = jnp.exp(jax.random.uniform(random_keys[1], (RELAY_SECTIONS, 1, HEAD_TOTAL), minval=math.log(1.0 / TOK_DEV), maxval=math.log(1.0 / 30.0)))
    baseline_rate = jnp.where(slow_heads, 0.25 / SEQUENCE_TOKENS, fast_rate)
    block_multiplier = jnp.exp(jax.random.uniform(random_keys[2], (RELAY_SECTIONS, SEQUENCE_TOKENS // TOK_DEV, 1, HEAD_TOTAL), minval=math.log(0.5), maxval=math.log(2.0)))
    block_multiplier = jnp.broadcast_to(block_multiplier, (RELAY_SECTIONS, SEQUENCE_TOKENS // TOK_DEV, TOK_DEV, HEAD_TOTAL)).reshape(RELAY_SECTIONS, SEQUENCE_TOKENS, HEAD_TOTAL)
    jitter_level = jax.random.uniform(random_keys[3], (RELAY_SECTIONS, SEQUENCE_TOKENS, HEAD_TOTAL), minval=0.5, maxval=1.5)
    spike_position = jax.random.randint(random_keys[4], (RELAY_SECTIONS, 2, HEAD_TOTAL), 0, SEQUENCE_TOKENS)
    spike_log_decay = jax.random.uniform(random_keys[5], (RELAY_SECTIONS, 2, HEAD_TOTAL), minval=math.log(0.5), maxval=math.log(0.8))
    spike_positions = jnp.arange(SEQUENCE_TOKENS)[None, :, None]
    spike_events = jnp.where(spike_positions == spike_position[:, 0:1, :], spike_log_decay[:, 0:1, :], 0.0) + jnp.where(spike_positions == spike_position[:, 1:2, :], spike_log_decay[:, 1:2, :], 0.0)
    return (-baseline_rate * block_multiplier * jitter_level + spike_events).astype(jnp.float32)


def block_scale(rng, extent, pieces, least, top_value):
    loudness, own = 1.0, jax.random.fold_in(rng, 6)
    for axis_at, shards_of in pieces:
        heights = jnp.exp(jax.random.uniform(jax.random.fold_in(own, axis_at), (shards_of,), jnp.float32, least / len(pieces), top_value / len(pieces)))
        loudness = loudness * jnp.repeat(heights, extent[axis_at] // shards_of).reshape([-1 if axis == axis_at else 1 for axis in range(len(extent))])
    return loudness


def centred(stream_key, extent, deviation, most, cuts=(), held_as=jnp.bfloat16):
    level = block_scale(stream_key, extent, cuts, -0.22, 0.18) if cuts else 1.0
    values = jax.random.normal(stream_key, extent, jnp.float32) * deviation * level
    return jnp.minimum(jnp.maximum(values, -most), most).astype(held_as)


def setup_inputs(seed: int = 0) -> dict:
    key_list = jax.random.split(jax.random.key(seed), 8)
    inputs = centred(key_list[0], (RELAY_SECTIONS, SEQUENCE_TOKENS, HEAD_TOTAL * P_SIZE), 1.0, 6.0, ((0, 8), (1, 32)))
    b_proj = centred(key_list[1], (RELAY_SECTIONS, SEQUENCE_TOKENS, N), 0.1, 0.59765625, ((0, 8), (1, 32)))
    c_proj = centred(key_list[2], (RELAY_SECTIONS, SEQUENCE_TOKENS, N), 0.1, 0.59765625, ((0, 8), (1, 32)))
    decay_log = draw_decay_log(jax.random.fold_in(key_list[7], 71), 0)
    level_weight = jnp.clip(jnp.exp(math.log(2.0) - 2.0794415 * jax.random.uniform(key_list[4], (RELAY_SECTIONS, SEQUENCE_TOKENS, LEVELS, HEAD_TOTAL), jnp.float32) ** block_scale(key_list[4], (RELAY_SECTIONS, SEQUENCE_TOKENS, LEVELS, HEAD_TOTAL), ((0, 8), (1, 32)), -0.2, 0.2)), 0.25, 2.0)
    out_grad = centred(key_list[5], (RELAY_SECTIONS, SEQUENCE_TOKENS, HEAD_TOTAL * P_SIZE), 1.0, 6.0, ((0, 8), (1, 32)))
    final_state_grad = centred(key_list[6], (RELAY_SECTIONS, HEAD_TOTAL, N, P_SIZE), (HEAD_TOTAL * P_SIZE) ** -0.5, 0.125, ((0, 8),), jnp.float32)
    return dict(inputs=inputs, b_proj=b_proj, c_proj=c_proj, decay_log=decay_log, level_weight=level_weight, out_grad=out_grad, final_state_grad=final_state_grad)


highest = lax.Precision.HIGHEST

def block_state(inputs, b_proj, decay_log):
    length, head_count = decay_log.shape
    running = jnp.cumsum(decay_log, axis=0)
    block_total = running[-1]
    factor = jnp.exp(block_total[None, :] - running)
    weighted = inputs.astype(jnp.float32).reshape(length, head_count, -1) * factor[:, :, None]
    state = jnp.einsum('tn,thp->hnp', b_proj.astype(jnp.float32), weighted, precision=highest)
    return (state, block_total)

def block_mixer(inputs, b_proj, c_proj, decay_log, level_weight, carries):
    length, head_count = decay_log.shape
    running = jnp.cumsum(decay_log, axis=0)
    values = inputs.astype(jnp.float32).reshape(length, head_count, -1)
    b_full = b_proj.astype(jnp.float32)
    c_full = c_proj.astype(jnp.float32)
    scores = jnp.dot(c_full, b_full.T, precision=highest)
    causal = jnp.arange(length)[:, None] >= jnp.arange(length)[None, :]
    spread = running[:, None, :] - running[None, :, :]
    decays = jnp.exp(jnp.where(causal[:, :, None], spread, -jnp.inf))
    mixing = decays * scores[:, :, None]
    local_part = jnp.einsum('tsh,shp->thp', mixing, values, precision=highest)
    result = level_weight[:, 0, :, None] * local_part
    lift = jnp.exp(running)
    for level_index in range(carries.shape[0]):
        reach = jnp.einsum('tn,hnp->thp', c_full, carries[level_index], precision=highest)
        result = result + (level_weight[:, level_index + 1, :] * lift)[:, :, None] * reach
    return result.reshape(length, -1)

def fenwick_carries(states, totals):
    blocks = totals.shape[0]
    inclusive = jnp.cumsum(totals, axis=0)
    before = inclusive - totals
    target = jnp.arange(blocks)[:, None]
    source = jnp.arange(blocks)[None, :]
    gaps = before[:, None, :] - inclusive[None, :, :]
    result = []
    for level_index in range(BITS):
        width = 2 ** level_index
        base = target // (2 * width) * (2 * width)
        member = (source >= base) & (source < base + width) & (target // width % 2 == 1)
        weights = jnp.exp(jnp.where(member[:, :, None], gaps, -jnp.inf))
        result.append(jnp.einsum('deh,ehnp->dhnp', weights, states, precision=highest))
    after = inclusive[-1][None, :] - inclusive
    final_state = jnp.einsum('eh,ehnp->hnp', jnp.exp(after), states, precision=highest)
    return (jnp.stack(result, axis=1), final_state)

def state_step(operands):
    return block_state(operands[0], operands[1], operands[2])

def mixer_step(operands):
    return block_mixer(operands[0], operands[1], operands[2], operands[3], operands[4], operands[5])

def section_forward(inputs_full, b_full, c_full, decay_full, weight_full):
    inputs_blocks = inputs_full.reshape(N_SEQ, TOK_DEV, -1)
    b_blocks = b_full.reshape(N_SEQ, TOK_DEV, -1)
    c_blocks = c_full.reshape(N_SEQ, TOK_DEV, -1)
    decay_blocks = decay_full.reshape(N_SEQ, TOK_DEV, -1)
    weight_blocks = weight_full.reshape(N_SEQ, TOK_DEV, LEVELS, -1)
    states, totals = lax.map(jax.checkpoint(state_step), (inputs_blocks, b_blocks, decay_blocks))
    carries, final_state = fenwick_carries(states, totals)
    mixed = lax.map(jax.checkpoint(mixer_step), (inputs_blocks, b_blocks, c_blocks, decay_blocks, weight_blocks, carries))
    return (mixed.reshape(SEQUENCE_TOKENS, -1), final_state)

def reference(inputs, b_proj, c_proj, decay_log, level_weight, out_grad, final_state_grad):
    input_list = []
    b_list = []
    c_list = []
    decay_list = []
    weight_list = []
    for section_index in range(RELAY_SECTIONS):
        unused, pull = jax.vjp(section_forward, inputs[section_index].astype(jnp.float32), b_proj[section_index].astype(jnp.float32), c_proj[section_index].astype(jnp.float32), decay_log[section_index], level_weight[section_index])
        grads = pull((out_grad[section_index].astype(jnp.float32), final_state_grad[section_index]))
        input_list.append(grads[0])
        b_list.append(grads[1])
        c_list.append(grads[2])
        decay_list.append(grads[3])
        weight_list.append(grads[4])
    input_grad = jnp.stack(input_list)
    upstream_grad = jnp.roll(input_grad, -1, axis=0).astype(jnp.bfloat16)
    return (upstream_grad, jnp.stack(b_list), jnp.stack(c_list), jnp.stack(decay_list), jnp.stack(weight_list))
```

```python
import jax
import jax.numpy as jnp
from jax import lax
from jax.experimental import pallas as pl
from jax.experimental.pallas import tpu as pltpu
from jax.sharding import PartitionSpec as P

MESH = pl.DeviceIdType.MESH
F32, BF16 = jnp.float32, jnp.bfloat16
BLK = 128
NB = 4
NZ = 8
HEADS = 32
HQ = HEADS // NB
HP = 64
N = 128
TOK = NB * BLK
COLS = HQ * HP
SECTIONS = 8
DEC, LWT, CPR, GRD, BPR, INP = range(6)
TOT, DZK, STA, DST, ZKK, DTT = 0, 1, 4, 5, 6, 9


def level_of(low, high):
    return (low ^ high).bit_length() - 1


def split(value):
    high = value.astype(BF16)
    return high, (value - high.astype(F32)).astype(BF16)


def mm(a, b):
    return jnp.dot(a, b, preferred_element_type=F32)


def mm_split(a, b16):
    high, low = split(a)
    return mm(high, b16) + mm(low, b16)


def lanes_sum(value, tri):
    first = value.astype(BF16)
    rest = value - first.astype(F32)
    second = rest.astype(BF16)
    third = (rest - second.astype(F32)).astype(BF16)
    return mm(first, tri) + mm(second, tri) + mm(third, tri)


def kernel(
    x_hbm, g_hbm, b_hbm, c_hbm, dec_hbm, lw_hbm, fsg_hbm,
    up_out, db_out, dc_out, wg_out, dg_out,
    xa, ga, ba, ca, dec, lw, fsg,
    xt, gt, gt16, bt16, ct16,
    r_rows, e_rows, f_rows, a_rows, w_rows,
    ag, fx, sp, dp, attn, ups,
    dz, st, tot, dzi, sti, dso, zko, dto, dsf, zkf, dti,
    wg, dct, dbs, dcs, dbi, dci, wgs, dgs, xdx,
    a_send, a_recv, z_send, z_recv, u_send, u_recv, o_send, o_recv, loc,
):
    seq = lax.axis_index("seq")
    sec = lax.axis_index("section")
    z = seq // NB
    q = lax.rem(seq, NB)
    before = lax.rem(sec + SECTIONS - 1, SECTIONS)
    after = lax.rem(sec + 1, SECTIONS)

    def at(zz, qq, section=sec):
        return {"seq": zz * NB + qq, "section": section}

    def remote(src, dst, send_sem, recv_sem, where):
        return pltpu.make_async_remote_copy(
            src_ref=src, dst_ref=dst, send_sem=send_sem, recv_sem=recv_sem,
            device_id=where, device_id_type=MESH,
        )

    barrier = pltpu.get_barrier_semaphore()

    def greet(where):
        pl.semaphore_signal(barrier, inc=1, device_id=where, device_id_type=MESH)

    for o in range(1, NB):
        greet(at(z, lax.rem(q + o, NB)))
    for o in range(1, NZ):
        greet(at(lax.rem(z + o, NZ), q))
    for i in range(NB):
        greet(at(z, i, before))
        greet(at(z, i, after))
    pl.semaphore_wait(barrier, NB - 1 + NZ - 1 + 2 * NB)

    def piece(kind, owner, slot):
        heads = pl.ds(pl.multiple_of(owner * HQ, HQ), HQ)
        cols = pl.ds(pl.multiple_of(owner * COLS, COLS), COLS)
        rows = pl.ds(pl.multiple_of(slot * BLK, BLK), BLK)
        if kind == DEC:
            return dec_hbm.at[heads, :], dec.at[slot]
        if kind == LWT:
            return lw_hbm.at[:, heads, :], lw.at[slot]
        if kind == CPR:
            return c_hbm, ca.at[rows, :]
        if kind == GRD:
            return g_hbm.at[:, cols], ga.at[rows, :]
        if kind == BPR:
            return b_hbm, ba.at[rows, :]
        return x_hbm.at[:, cols], xa.at[rows, :]

    def group_send(kind, o):
        peer = lax.rem(q + o, NB)
        src, dst = piece(kind, peer, q)
        return remote(src, dst, a_send.at[kind, o], a_recv.at[kind, q], at(z, peer))

    def group_start(kind):
        for o in range(1, NB):
            group_send(kind, o).start()
        src, dst = piece(kind, q, q)
        pltpu.make_async_copy(src, dst, loc.at[kind]).start()

    def group_wait(kind):
        src, dst = piece(kind, q, q)
        pltpu.make_async_copy(src, dst, loc.at[kind]).wait()
        for o in range(1, NB):
            peer = lax.rem(q + o, NB)
            dst = piece(kind, peer, peer)[1]
            remote(dst, dst, a_send.at[kind, o], a_recv.at[kind, peer], at(z, peer)).wait_recv()

    for kind in (DEC, LWT, CPR, GRD, BPR, INP):
        group_start(kind)
    final_copy = pltpu.make_async_copy(fsg_hbm.at[q * HQ + z], fsg, loc.at[6])
    final_copy.start()

    row_of = lax.broadcasted_iota(jnp.int32, (BLK, BLK), 0)
    col_of = lax.broadcasted_iota(jnp.int32, (BLK, BLK), 1)
    causal = row_of <= col_of
    upto = jnp.where(causal, 1.0, 0.0).astype(BF16)
    onward = jnp.where(row_of >= col_of, 1.0, 0.0).astype(BF16)
    left = lax.broadcasted_iota(jnp.int32, (BLK, BLK), 1) < HP

    group_wait(DEC)
    running = lanes_sum(jnp.concatenate([dec[i] for i in range(NB)], axis=0), upto)
    sofar = jnp.zeros((HQ, 1), F32)
    for i in range(NB):
        own = running[i * HQ : (i + 1) * HQ]
        r_rows[:, i * BLK : (i + 1) * BLK] = own + sofar
        sofar = sofar + own[:, BLK - 1 : BLK]
    tot[z] = jnp.broadcast_to(sofar, (HQ, BLK))

    def z_send_one(kind, o, src, dst, slot_kind=None):
        peer = lax.rem(z + o, NZ)
        return remote(src, dst, z_send.at[kind, o], z_recv.at[kind, z], at(peer, q))

    def z_wait(kind, dst, peer):
        remote(dst, dst, z_send.at[kind, 0], z_recv.at[kind, peer], at(peer, q)).wait_recv()

    @pl.loop(1, NZ)
    def _(o):
        z_send_one(TOT, o, tot.at[z], tot.at[z]).start()

    r_all = r_rows[...]
    e_rows[...] = jnp.exp(r_all)
    f_rows[...] = jnp.exp(sofar - r_all)
    group_wait(LWT)
    for k in range(3):
        for i in range(NB):
            a_rows[k, :, i * BLK : (i + 1) * BLK] = lw[i, 3 + k] * e_rows[:, i * BLK : (i + 1) * BLK]
    for i in range(NB):
        for j in range(i, NB):
            w_rows[i, :, j * BLK : (j + 1) * BLK] = lw[j, level_of(i, j) + 1]

    group_wait(CPR)
    for i in range(NB):
        ct16[:, i * BLK : (i + 1) * BLK] = ca[i * BLK : (i + 1) * BLK, :].astype(F32).T.astype(BF16)
    wg[...] = jnp.zeros_like(wg)
    dct[...] = jnp.zeros_like(dct)
    dp[...] = jnp.zeros_like(dp)

    group_wait(GRD)

    @pl.loop(0, NB)
    def _(c):
        cols = pl.ds(pl.multiple_of(c * BLK, BLK), BLK)
        for i in range(NB):
            rows = ga[i * BLK : (i + 1) * BLK, cols].astype(F32).T
            gt[cols, i * BLK : (i + 1) * BLK] = rows
            gt16[cols, i * BLK : (i + 1) * BLK] = rows.astype(BF16)

    def bit(zz, k):
        return lax.rem(zz // 2**k, 2) == 1

    def head_rows(h):
        return pl.ds(pl.multiple_of(h * HP, HP), HP)

    for k in range(3):

        @pl.when(bit(z, k))
        def _(k=k):
            @pl.loop(0, HQ)
            def _(h):
                high, low = split(gt[head_rows(h), :] * a_rows[k, pl.ds(h, 1), :])
                ag[k, 0, head_rows(h), :] = high
                ag[k, 1, head_rows(h), :] = low

            dz[k] = mm(ag[k, 0], ca[...]) + mm(ag[k, 1], ca[...])
            dzi[k, z] = dz[k, head_rows(z), :]

            @pl.loop(1, NZ)
            def _(o):
                peer = lax.rem(z + o, NZ)
                z_send_one(DZK + k, o, dz.at[k, head_rows(peer), :], dzi.at[k, z]).start()

    group_wait(BPR)
    for i in range(NB):
        bt16[:, i * BLK : (i + 1) * BLK] = ba[i * BLK : (i + 1) * BLK, :].astype(F32).T.astype(BF16)
    group_wait(INP)

    @pl.loop(0, NB)
    def _(c):
        cols = pl.ds(pl.multiple_of(c * BLK, BLK), BLK)
        for i in range(NB):
            xt[cols, i * BLK : (i + 1) * BLK] = xa[i * BLK : (i + 1) * BLK, cols].astype(F32).T

    @pl.loop(0, HQ)
    def _(h):
        high, low = split(xt[head_rows(h), :] * f_rows[pl.ds(h, 1), :])
        fx[0, head_rows(h), :] = high
        fx[1, head_rows(h), :] = low

    st[...] = mm(fx[0], ba[...]) + mm(fx[1], ba[...])
    sti[z] = st[head_rows(z), :]

    @pl.loop(1, NZ)
    def _(o):
        peer = lax.rem(z + o, NZ)
        z_send_one(STA, o, st.at[head_rows(peer), :], sti.at[z]).start()

    sp[...] = mm(ba[...], ct16[...])

    @pl.loop(0, NB)
    def _(p):
        cols = pl.ds(pl.multiple_of(p * BLK, BLK), BLK)
        runs = [r_rows[pl.ds(2 * p + half, 1), :] for half in range(2)]
        found = [{(level, j): jnp.zeros((1, BLK), F32) for level in range(3) for j in range(NB)} for _ in range(2)]
        for i in range(NB):
            keys = slice(i * BLK, (i + 1) * BLK)
            pair = []
            for half in range(2):
                keep = left if half == 0 else jnp.logical_not(left)
                own = jnp.where(keep, xa[keys, cols].astype(F32), 0.0).astype(BF16)
                run = runs[half]
                weights = w_rows[i, pl.ds(2 * p + half, 1), :]
                r_keys = jnp.broadcast_to(run[:, keys], (BLK, BLK)).T
                grad = jnp.zeros((BLK, BLK), F32)
                for j in range(i, NB):
                    queries = slice(j * BLK, (j + 1) * BLK)
                    product = mm(own, gt16[cols, queries])
                    spread = run[:, queries] - r_keys
                    if i == j:
                        spread = jnp.where(causal, spread, -1e30)
                    decay = jnp.exp(spread)
                    score = sp[keys, queries]
                    level = level_of(i, j) + 1
                    found[half][level, j] += jnp.sum(product * decay * score, axis=0, keepdims=True)
                    decay = decay * weights[:, queries]
                    dp[keys, queries] += product * decay
                    grad = grad + mm_split(score * decay, ga[queries, cols])
                pair.append(grad)
            attn[cols, keys] = jnp.where(left, pair[0], pair[1]).T
        for half in range(2):
            for level in range(3):
                row = jnp.concatenate([found[half][level, j] for j in range(NB)], axis=1)
                wg[level, pl.ds(2 * p + half, 1), :] = row

    @pl.loop(1, NZ)
    def _(o):
        peer = lax.rem(z + o, NZ)
        z_wait(TOT, tot.at[peer], peer)

    for k in range(3):

        @pl.loop(1, NZ)
        def _(o, k=k):
            peer = lax.rem(z + o, NZ)

            @pl.when(bit(peer, k))
            def _():
                z_wait(DZK + k, dzi.at[k, peer], peer)

    final_copy.wait()
    totals = [tot[d, pl.ds(z, 1), :] for d in range(NZ)]
    weight = {}
    for e in range(NZ):
        gap = jnp.zeros((1, BLK), F32)
        for d in range(e + 1, NZ):
            weight[e, d] = jnp.exp(gap)
            gap = gap + totals[d]
        weight[e, NZ] = jnp.exp(gap)
    for e in range(NZ):
        grad = weight[e, NZ] * fsg[...]
        for d in range(e + 1, NZ):
            grad = grad + weight[e, d] * dzi[level_of(e, d), d]
        dso[e] = grad

    dsf[head_rows(z), :] = dso[z]

    @pl.loop(1, NZ)
    def _(o):
        peer = lax.rem(z + o, NZ)
        z_send_one(DST, o, dso.at[peer], dsf.at[head_rows(z), :]).start()

    @pl.loop(1, NZ)
    def _(o):
        peer = lax.rem(z + o, NZ)
        z_wait(STA, sti.at[peer], peer)

    for d in range(1, NZ):
        for k in range(3):
            if d >> k & 1:
                base = d - d % 2 ** (k + 1)
                carry = jnp.zeros((HP, N), F32)
                for e in range(base, base + 2**k):
                    carry = carry + weight[e, d] * sti[e]
                zko[k, d] = carry

    for k in range(3):

        @pl.when(bit(z, k))
        def _(k=k):
            zkf[k, head_rows(z), :] = zko[k, z]

        @pl.loop(1, NZ)
        def _(o, k=k):
            peer = lax.rem(z + o, NZ)

            @pl.when(bit(peer, k))
            def _():
                z_send_one(ZKK + k, o, zko.at[k, peer], zkf.at[k, head_rows(z), :]).start()

    def fold(value):
        return sum(value[8 * i : 8 * (i + 1)] for i in range(HP // 8))

    across = [jnp.zeros((8, N), F32) for _ in range(NZ)]
    for e in range(NZ):
        for d in range(e + 1, NZ + 1):
            other = fsg[...] if d == NZ else dzi[level_of(e, d), d]
            shared = weight[e, d] * fold(sti[e] * other)
            for f in range(e, d):
                across[f] = across[f] + shared
    for f in range(NZ):
        dto[f] = across[f]
    dti[z] = dto[z]

    @pl.loop(1, NZ)
    def _(o):
        peer = lax.rem(z + o, NZ)
        z_send_one(DTT, o, dto.at[peer], dti.at[z]).start()

    @pl.loop(1, NZ)
    def _(o):
        peer = lax.rem(z + o, NZ)
        z_wait(DST, dsf.at[head_rows(peer), :], peer)

    @pl.loop(0, NB)
    def _(p):
        cols = pl.ds(pl.multiple_of(p * BLK, BLK), BLK)
        spread = mm_split(dsf[cols, :], bt16[...])
        factor = jnp.concatenate(
            [jnp.broadcast_to(f_rows[pl.ds(2 * p + half, 1), :], (HP, TOK)) for half in range(2)], axis=0
        )
        grad = attn[cols, :] + factor * spread
        own = grad * xt[cols, :]
        for half in range(2):
            xdx[pl.ds(2 * p + half, 1), :] = jnp.sum(own[half * HP : (half + 1) * HP], axis=0, keepdims=True)
        for i in range(NB):
            ups[i * BLK : (i + 1) * BLK, cols] = grad[:, i * BLK : (i + 1) * BLK].T.astype(BF16)

    def up_send(i):
        there = up_out.at[:, pl.ds(pl.multiple_of(q * COLS, COLS), COLS)]
        return remote(ups.at[i * BLK : (i + 1) * BLK, :], there, u_send.at[i], u_recv.at[q], at(z, i, before))

    for i in range(NB):
        up_send(i).start()

    db_t = jnp.zeros((N, TOK), F32)
    high, low = split(jnp.concatenate([dsf[c * BLK : (c + 1) * BLK, :].T for c in range(NB)], axis=1))
    db_t = mm(high, fx[0]) + mm(low, fx[0]) + mm(high, fx[1])
    for i in range(NB):
        keys = slice(i * BLK, (i + 1) * BLK)
        dbs[i] = mm_split(dp[keys, :], ca[...]) + db_t[:, keys].T

    def sum_send(kind, o):
        peer = lax.rem(q + o, NB)
        src, dst = ((dbs, dbi), (dcs, dci))[kind]
        return remote(src.at[peer], dst.at[q], o_send.at[kind, o], o_recv.at[kind, q], at(z, peer))

    for o in range(1, NB):
        sum_send(0, o).start()
    dbi[q] = dbs[q]

    for k in range(3):

        @pl.when(bit(z, k))
        def _(k=k):
            @pl.loop(1, NZ)
            def _(o):
                peer = lax.rem(z + o, NZ)
                z_wait(ZKK + k, zkf.at[k, head_rows(peer), :], peer)

            @pl.loop(0, NB)
            def _(p):
                cols = pl.ds(pl.multiple_of(p * BLK, BLK), BLK)
                reach = mm_split(zkf[k, cols, :], ct16[...]) * gt[cols, :]
                for half in range(2):
                    h = 2 * p + half
                    row = jnp.sum(reach[half * HP : (half + 1) * HP], axis=0, keepdims=True)
                    wg[3 + k, pl.ds(h, 1), :] = row * e_rows[pl.ds(h, 1), :]

            high, low = split(jnp.concatenate([zkf[k, c * BLK : (c + 1) * BLK, :].T for c in range(NB)], axis=1))
            dct[...] += mm(high, ag[k, 0]) + mm(low, ag[k, 0]) + mm(high, ag[k, 1])

    high, low = split(dp[...])
    dc_t = dct[...] + mm(bt16[...], high) + mm(bt16[...], low)
    for i in range(NB):
        dcs[i] = dc_t[:, i * BLK : (i + 1) * BLK].T
    for o in range(1, NB):
        sum_send(1, o).start()
    dci[q] = dcs[q]

    @pl.loop(1, NZ)
    def _(o):
        peer = lax.rem(z + o, NZ)
        z_wait(DTT, dti.at[peer], peer)

    later = jnp.sum(
        jnp.concatenate([jnp.sum(dti[h], axis=0, keepdims=True) for h in range(HQ)], axis=0), axis=1, keepdims=True
    )
    pieces = []
    for i in range(NB):
        here = slice(i * BLK, (i + 1) * BLK)
        change = -xdx[:, here]
        for level in range(6):
            change = change + lw[i, level] * wg[level, :, here]
            wgs[i, level] = wg[level, :, here]
        pieces.append(change)
    sums = lanes_sum(jnp.concatenate(pieces, axis=0), onward)
    for i in reversed(range(NB)):
        own = sums[i * HQ : (i + 1) * HQ]
        dgs[i] = own + later
        later = later + own[:, :1]

    mine = pl.ds(pl.multiple_of(q * HQ, HQ), HQ)

    def rows_send(kind, o):
        peer = lax.rem(q + o, NB)
        src, dst = (wgs.at[peer], wg_out.at[:, mine, :]) if kind == 2 else (dgs.at[peer], dg_out.at[mine, :])
        return remote(src, dst, o_send.at[kind, o], o_recv.at[kind, q], at(z, peer))

    for o in range(1, NB):
        rows_send(2, o).start()
        rows_send(3, o).start()
    own_wg = pltpu.make_async_copy(wgs.at[q], wg_out.at[:, mine, :], loc.at[7])
    own_dg = pltpu.make_async_copy(dgs.at[q], dg_out.at[mine, :], loc.at[8])
    own_wg.start()
    own_dg.start()

    for kind, landed in ((0, dbi), (1, dci)):
        for o in range(1, NB):
            peer = lax.rem(q + o, NB)
            there = landed.at[peer]
            remote(there, there, o_send.at[kind, o], o_recv.at[kind, peer], at(z, peer)).wait_recv()
    db_out[...] = dbi[0] + dbi[1] + dbi[2] + dbi[3]
    dc_out[...] = dci[0] + dci[1] + dci[2] + dci[3]

    own_wg.wait()
    own_dg.wait()
    for o in range(1, NB):
        peer = lax.rem(q + o, NB)
        theirs = pl.ds(pl.multiple_of(peer * HQ, HQ), HQ)
        for kind, there in ((2, wg_out.at[:, theirs, :]), (3, dg_out.at[theirs, :])):
            remote(there, there, o_send.at[kind, o], o_recv.at[kind, peer], at(z, peer)).wait_recv()
    for i in range(NB):
        there = up_out.at[:, i * COLS : (i + 1) * COLS]
        remote(there, there, u_send.at[i], u_recv.at[i], at(z, i, before)).wait_recv()

    for kind in range(6):
        for o in range(1, NB):
            group_send(kind, o).wait_send()
    for i in range(NB):
        up_send(i).wait_send()
    for o in range(1, NB):
        sum_send(0, o).wait_send()
        sum_send(1, o).wait_send()
        rows_send(2, o).wait_send()
        rows_send(3, o).wait_send()

    @pl.loop(1, NZ)
    def _(o):
        peer = lax.rem(z + o, NZ)
        z_send_one(TOT, o, tot.at[z], tot.at[z]).wait_send()
        z_send_one(STA, o, st.at[head_rows(peer), :], sti.at[z]).wait_send()
        z_send_one(DST, o, dso.at[peer], dsf.at[head_rows(z), :]).wait_send()
        z_send_one(DTT, o, dto.at[peer], dti.at[z]).wait_send()
        for k in range(3):

            @pl.when(bit(z, k))
            def _(k=k):
                z_send_one(DZK + k, o, dz.at[k, head_rows(peer), :], dzi.at[k, z]).wait_send()

            @pl.when(bit(peer, k))
            def _(k=k):
                z_send_one(ZKK + k, o, zko.at[k, peer], zkf.at[k, head_rows(z), :]).wait_send()


def body(inputs, b_proj, c_proj, decay_log, level_weight, out_grad, final_state_grad):
    def vmem(*shape, dtype=F32):
        return pltpu.VMEM(shape, dtype)

    scratch = [
        vmem(TOK, COLS, dtype=BF16),
        vmem(TOK, COLS, dtype=BF16),
        vmem(TOK, N, dtype=BF16),
        vmem(TOK, N, dtype=BF16),
        vmem(NB, HQ, BLK),
        vmem(NB, 6, HQ, BLK),
        vmem(HP, N),
        vmem(COLS, TOK),
        vmem(COLS, TOK),
        vmem(COLS, TOK, dtype=BF16),
        vmem(N, TOK, dtype=BF16),
        vmem(N, TOK, dtype=BF16),
        vmem(HQ, TOK),
        vmem(HQ, TOK),
        vmem(HQ, TOK),
        vmem(3, HQ, TOK),
        vmem(NB, HQ, TOK),
        vmem(3, 2, COLS, TOK, dtype=BF16),
        vmem(2, COLS, TOK, dtype=BF16),
        vmem(TOK, TOK),
        vmem(TOK, TOK),
        vmem(COLS, TOK),
        vmem(TOK, COLS, dtype=BF16),
        vmem(3, COLS, N),
        vmem(COLS, N),
        vmem(NZ, HQ, BLK),
        vmem(3, NZ, HP, N),
        vmem(NZ, HP, N),
        vmem(NZ, HP, N),
        vmem(3, NZ, HP, N),
        vmem(NZ, 8, N),
        vmem(COLS, N),
        vmem(3, COLS, N),
        vmem(NZ, 8, N),
        vmem(6, HQ, TOK),
        vmem(N, TOK),
        vmem(NB, BLK, N),
        vmem(NB, BLK, N),
        vmem(NB, BLK, N),
        vmem(NB, BLK, N),
        vmem(NB, 6, HQ, BLK),
        vmem(NB, HQ, BLK),
        vmem(HQ, TOK),
        pltpu.SemaphoreType.DMA((6, NB)),
        pltpu.SemaphoreType.DMA((6, NB)),
        pltpu.SemaphoreType.DMA((10, NZ)),
        pltpu.SemaphoreType.DMA((10, NZ)),
        pltpu.SemaphoreType.DMA((NB,)),
        pltpu.SemaphoreType.DMA((NB,)),
        pltpu.SemaphoreType.DMA((4, NB)),
        pltpu.SemaphoreType.DMA((4, NB)),
        pltpu.SemaphoreType.DMA((9,)),
    ]
    anywhere = pl.BlockSpec(memory_space=pl.ANY)
    near = pl.BlockSpec(memory_space=pltpu.VMEM)
    up, db, dc, wg, dg = pl.pallas_call(
        kernel,
        out_shape=(
            jax.ShapeDtypeStruct((BLK, HEADS * HP), BF16),
            jax.ShapeDtypeStruct((BLK, N), F32),
            jax.ShapeDtypeStruct((BLK, N), F32),
            jax.ShapeDtypeStruct((6, HEADS, BLK), F32),
            jax.ShapeDtypeStruct((HEADS, BLK), F32),
        ),
        in_specs=[anywhere] * 7,
        out_specs=(anywhere, near, near, anywhere, anywhere),
        scratch_shapes=scratch,
        compiler_params=pltpu.CompilerParams(
            collective_id=0, has_side_effects=True, vmem_limit_bytes=40 * 2**20
        ),
    )(
        inputs[0],
        out_grad[0],
        b_proj[0],
        c_proj[0],
        decay_log[0].T,
        jnp.transpose(level_weight[0], (1, 2, 0)),
        jnp.transpose(final_state_grad[0], (0, 2, 1)),
    )
    return (up[None], db[None], dc[None], dg.T[None], jnp.transpose(wg, (2, 0, 1))[None])


def solution(mesh):
    rows = P("section", "seq", None)
    deep = P("section", "seq", None, None)
    return jax.shard_map(
        body,
        mesh=mesh,
        in_specs=(rows, rows, rows, rows, deep, rows, P("section", None, None, None)),
        out_specs=(rows, rows, rows, rows, deep),
        check_vma=False,
    )
```

```python
import jax
import jax.numpy as jnp
from jax import lax
from jax.experimental import pallas as pl
from jax.experimental.pallas import tpu as pltpu
from jax.sharding import PartitionSpec as P

MESH = pl.DeviceIdType.MESH
F32, BF16 = jnp.float32, jnp.bfloat16
BLK = 128
NB = 4
NZ = 8
HEADS = 32
HQ = HEADS // NB
HP = 64
N = 128
TOK = NB * BLK
COLS = HQ * HP
SECTIONS = 8
DEC, LWT, CPR, GRD, BPR, INP = range(6)
TOT, DZK, STA, DST, ZKK, DTT = 0, 1, 4, 5, 6, 9


def level_of(low, high):
    return (low ^ high).bit_length() - 1


def split(value):
    high = value.astype(BF16)
    return high, (value - high.astype(F32)).astype(BF16)


def mm(a, b):
    return jnp.dot(a, b, preferred_element_type=F32)


def mm_split(a, b16):
    high, low = split(a)
    return mm(high, b16) + mm(low, b16)


def lanes_sum(value, tri):
    first = value.astype(BF16)
    rest = value - first.astype(F32)
    second = rest.astype(BF16)
    third = (rest - second.astype(F32)).astype(BF16)
    return mm(first, tri) + mm(second, tri) + mm(third, tri)


def kernel(
    x_hbm, g_hbm, b_hbm, c_hbm, dec_hbm, lw_hbm, fsg_hbm,
    up_out, db_out, dc_out, wg_out, dg_out,
    xa, ga, ba, ca, dec, lw, fsg,
    xt, gt, gt16, bt16, ct16,
    r_rows, e_rows, f_rows, a_rows, w_rows,
    ag, fx, sp, dp, attn, ups,
    dz, st, tot, dzi, sti, dso, zko, dto, dsf, zkf, dti,
    wg, dct, dbs, dcs, dbi, dci, wgs, dgs, xdx,
    a_send, a_recv, z_send, z_recv, u_send, u_recv, o_send, o_recv, loc,
):
    seq = lax.axis_index("seq")
    sec = lax.axis_index("section")
    z = seq // NB
    q = lax.rem(seq, NB)
    before = lax.rem(sec + SECTIONS - 1, SECTIONS)
    after = lax.rem(sec + 1, SECTIONS)

    def at(zz, qq, section=sec):
        return {"seq": zz * NB + qq, "section": section}

    def remote(src, dst, send_sem, recv_sem, where):
        return pltpu.make_async_remote_copy(
            src_ref=src, dst_ref=dst, send_sem=send_sem, recv_sem=recv_sem,
            device_id=where, device_id_type=MESH,
        )

    barrier = pltpu.get_barrier_semaphore()

    def greet(where):
        pl.semaphore_signal(barrier, inc=1, device_id=where, device_id_type=MESH)

    for o in range(1, NB):
        greet(at(z, lax.rem(q + o, NB)))
    for o in range(1, NZ):
        greet(at(lax.rem(z + o, NZ), q))
    for i in range(NB):
        greet(at(z, i, before))
        greet(at(z, i, after))
    pl.semaphore_wait(barrier, NB - 1 + NZ - 1 + 2 * NB)

    def piece(kind, owner, slot):
        heads = pl.ds(pl.multiple_of(owner * HQ, HQ), HQ)
        cols = pl.ds(pl.multiple_of(owner * COLS, COLS), COLS)
        rows = pl.ds(pl.multiple_of(slot * BLK, BLK), BLK)
        if kind == DEC:
            return dec_hbm.at[heads, :], dec.at[slot]
        if kind == LWT:
            return lw_hbm.at[:, heads, :], lw.at[slot]
        if kind == CPR:
            return c_hbm, ca.at[rows, :]
        if kind == GRD:
            return g_hbm.at[:, cols], ga.at[rows, :]
        if kind == BPR:
            return b_hbm, ba.at[rows, :]
        return x_hbm.at[:, cols], xa.at[rows, :]

    def group_send(kind, o):
        peer = lax.rem(q + o, NB)
        src, dst = piece(kind, peer, q)
        return remote(src, dst, a_send.at[kind, o], a_recv.at[kind, q], at(z, peer))

    def group_start(kind):
        for o in range(1, NB):
            group_send(kind, o).start()
        src, dst = piece(kind, q, q)
        pltpu.make_async_copy(src, dst, loc.at[kind]).start()

    def group_wait(kind):
        src, dst = piece(kind, q, q)
        pltpu.make_async_copy(src, dst, loc.at[kind]).wait()
        for o in range(1, NB):
            peer = lax.rem(q + o, NB)
            dst = piece(kind, peer, peer)[1]
            remote(dst, dst, a_send.at[kind, o], a_recv.at[kind, peer], at(z, peer)).wait_recv()

    for kind in (DEC, LWT, CPR, GRD):
        group_start(kind)
    final_copy = pltpu.make_async_copy(fsg_hbm.at[q * HQ + z], fsg, loc.at[6])
    final_copy.start()

    row_of = lax.broadcasted_iota(jnp.int32, (BLK, BLK), 0)
    col_of = lax.broadcasted_iota(jnp.int32, (BLK, BLK), 1)
    causal = row_of <= col_of
    upto = jnp.where(causal, 1.0, 0.0).astype(BF16)
    onward = jnp.where(row_of >= col_of, 1.0, 0.0).astype(BF16)
    left = lax.broadcasted_iota(jnp.int32, (BLK, BLK), 1) < HP

    group_wait(DEC)
    running = lanes_sum(jnp.concatenate([dec[i] for i in range(NB)], axis=0), upto)
    sofar = jnp.zeros((HQ, 1), F32)
    for i in range(NB):
        own = running[i * HQ : (i + 1) * HQ]
        r_rows[:, i * BLK : (i + 1) * BLK] = own + sofar
        sofar = sofar + own[:, BLK - 1 : BLK]
    tot[z] = jnp.broadcast_to(sofar, (HQ, BLK))

    def z_send_one(kind, o, src, dst, slot_kind=None):
        peer = lax.rem(z + o, NZ)
        return remote(src, dst, z_send.at[kind, o], z_recv.at[kind, z], at(peer, q))

    def z_wait(kind, dst, peer):
        remote(dst, dst, z_send.at[kind, 0], z_recv.at[kind, peer], at(peer, q)).wait_recv()

    @pl.loop(1, NZ)
    def _(o):
        z_send_one(TOT, o, tot.at[z], tot.at[z]).start()

    r_all = r_rows[...]
    e_rows[...] = jnp.exp(r_all)
    f_rows[...] = jnp.exp(sofar - r_all)
    group_wait(LWT)
    for k in range(3):
        for i in range(NB):
            a_rows[k, :, i * BLK : (i + 1) * BLK] = lw[i, 3 + k] * e_rows[:, i * BLK : (i + 1) * BLK]
    for i in range(NB):
        for j in range(i, NB):
            w_rows[i, :, j * BLK : (j + 1) * BLK] = lw[j, level_of(i, j) + 1]

    group_wait(CPR)
    for i in range(NB):
        ct16[:, i * BLK : (i + 1) * BLK] = ca[i * BLK : (i + 1) * BLK, :].astype(F32).T.astype(BF16)
    wg[...] = jnp.zeros_like(wg)
    dct[...] = jnp.zeros_like(dct)
    dp[...] = jnp.zeros_like(dp)

    group_wait(GRD)
    group_start(BPR)
    group_start(INP)

    @pl.loop(0, NB)
    def _(c):
        cols = pl.ds(pl.multiple_of(c * BLK, BLK), BLK)
        for i in range(NB):
            rows = ga[i * BLK : (i + 1) * BLK, cols].astype(F32).T
            gt[cols, i * BLK : (i + 1) * BLK] = rows
            gt16[cols, i * BLK : (i + 1) * BLK] = rows.astype(BF16)

    def bit(zz, k):
        return lax.rem(zz // 2**k, 2) == 1

    def head_rows(h):
        return pl.ds(pl.multiple_of(h * HP, HP), HP)

    for k in range(3):

        @pl.when(bit(z, k))
        def _(k=k):
            @pl.loop(0, HQ)
            def _(h):
                high, low = split(gt[head_rows(h), :] * a_rows[k, pl.ds(h, 1), :])
                ag[k, 0, head_rows(h), :] = high
                ag[k, 1, head_rows(h), :] = low

            dz[k] = mm(ag[k, 0], ca[...]) + mm(ag[k, 1], ca[...])
            dzi[k, z] = dz[k, head_rows(z), :]

            @pl.loop(1, NZ)
            def _(o):
                peer = lax.rem(z + o, NZ)
                z_send_one(DZK + k, o, dz.at[k, head_rows(peer), :], dzi.at[k, z]).start()

    group_wait(BPR)
    for i in range(NB):
        bt16[:, i * BLK : (i + 1) * BLK] = ba[i * BLK : (i + 1) * BLK, :].astype(F32).T.astype(BF16)
    group_wait(INP)

    @pl.loop(0, NB)
    def _(c):
        cols = pl.ds(pl.multiple_of(c * BLK, BLK), BLK)
        for i in range(NB):
            xt[cols, i * BLK : (i + 1) * BLK] = xa[i * BLK : (i + 1) * BLK, cols].astype(F32).T

    @pl.loop(0, HQ)
    def _(h):
        high, low = split(xt[head_rows(h), :] * f_rows[pl.ds(h, 1), :])
        fx[0, head_rows(h), :] = high
        fx[1, head_rows(h), :] = low

    st[...] = mm(fx[0], ba[...]) + mm(fx[1], ba[...])
    sti[z] = st[head_rows(z), :]

    @pl.loop(1, NZ)
    def _(o):
        peer = lax.rem(z + o, NZ)
        z_send_one(STA, o, st.at[head_rows(peer), :], sti.at[z]).start()

    sp[...] = mm(ba[...], ct16[...])

    @pl.loop(0, NB)
    def _(p):
        cols = pl.ds(pl.multiple_of(p * BLK, BLK), BLK)
        runs = [r_rows[pl.ds(2 * p + half, 1), :] for half in range(2)]
        found = [{(level, j): jnp.zeros((1, BLK), F32) for level in range(3) for j in range(NB)} for _ in range(2)]
        for i in range(NB):
            keys = slice(i * BLK, (i + 1) * BLK)
            pair = []
            for half in range(2):
                keep = left if half == 0 else jnp.logical_not(left)
                own = jnp.where(keep, xa[keys, cols].astype(F32), 0.0).astype(BF16)
                run = runs[half]
                weights = w_rows[i, pl.ds(2 * p + half, 1), :]
                r_keys = jnp.broadcast_to(run[:, keys], (BLK, BLK)).T
                grad = jnp.zeros((BLK, BLK), F32)
                for j in range(i, NB):
                    queries = slice(j * BLK, (j + 1) * BLK)
                    product = mm(own, gt16[cols, queries])
                    spread = run[:, queries] - r_keys
                    if i == j:
                        spread = jnp.where(causal, spread, -1e30)
                    decay = jnp.exp(spread)
                    score = sp[keys, queries]
                    level = level_of(i, j) + 1
                    found[half][level, j] += jnp.sum(product * decay * score, axis=0, keepdims=True)
                    decay = decay * weights[:, queries]
                    dp[keys, queries] += product * decay
                    grad = grad + mm_split(score * decay, ga[queries, cols])
                pair.append(grad)
            attn[cols, keys] = jnp.where(left, pair[0], pair[1]).T
        for half in range(2):
            for level in range(3):
                row = jnp.concatenate([found[half][level, j] for j in range(NB)], axis=1)
                wg[level, pl.ds(2 * p + half, 1), :] = row

    @pl.loop(1, NZ)
    def _(o):
        peer = lax.rem(z + o, NZ)
        z_wait(TOT, tot.at[peer], peer)

    for k in range(3):

        @pl.loop(1, NZ)
        def _(o, k=k):
            peer = lax.rem(z + o, NZ)

            @pl.when(bit(peer, k))
            def _():
                z_wait(DZK + k, dzi.at[k, peer], peer)

    final_copy.wait()
    totals = [tot[d, pl.ds(z, 1), :] for d in range(NZ)]
    weight = {}
    for e in range(NZ):
        gap = jnp.zeros((1, BLK), F32)
        for d in range(e + 1, NZ):
            weight[e, d] = jnp.exp(gap)
            gap = gap + totals[d]
        weight[e, NZ] = jnp.exp(gap)
    for e in range(NZ):
        grad = weight[e, NZ] * fsg[...]
        for d in range(e + 1, NZ):
            grad = grad + weight[e, d] * dzi[level_of(e, d), d]
        dso[e] = grad

    dsf[head_rows(z), :] = dso[z]

    @pl.loop(1, NZ)
    def _(o):
        peer = lax.rem(z + o, NZ)
        z_send_one(DST, o, dso.at[peer], dsf.at[head_rows(z), :]).start()

    @pl.loop(1, NZ)
    def _(o):
        peer = lax.rem(z + o, NZ)
        z_wait(STA, sti.at[peer], peer)

    for d in range(1, NZ):
        for k in range(3):
            if d >> k & 1:
                base = d - d % 2 ** (k + 1)
                carry = jnp.zeros((HP, N), F32)
                for e in range(base, base + 2**k):
                    carry = carry + weight[e, d] * sti[e]
                zko[k, d] = carry

    for k in range(3):

        @pl.when(bit(z, k))
        def _(k=k):
            zkf[k, head_rows(z), :] = zko[k, z]

        @pl.loop(1, NZ)
        def _(o, k=k):
            peer = lax.rem(z + o, NZ)

            @pl.when(bit(peer, k))
            def _():
                z_send_one(ZKK + k, o, zko.at[k, peer], zkf.at[k, head_rows(z), :]).start()

    def fold(value):
        return sum(value[8 * i : 8 * (i + 1)] for i in range(HP // 8))

    across = [jnp.zeros((8, N), F32) for _ in range(NZ)]
    for e in range(NZ):
        for d in range(e + 1, NZ + 1):
            other = fsg[...] if d == NZ else dzi[level_of(e, d), d]
            shared = weight[e, d] * fold(sti[e] * other)
            for f in range(e, d):
                across[f] = across[f] + shared
    for f in range(NZ):
        dto[f] = across[f]
    dti[z] = dto[z]

    @pl.loop(1, NZ)
    def _(o):
        peer = lax.rem(z + o, NZ)
        z_send_one(DTT, o, dto.at[peer], dti.at[z]).start()

    @pl.loop(1, NZ)
    def _(o):
        peer = lax.rem(z + o, NZ)
        z_wait(DST, dsf.at[head_rows(peer), :], peer)

    @pl.loop(0, NB)
    def _(p):
        cols = pl.ds(pl.multiple_of(p * BLK, BLK), BLK)
        spread = mm_split(dsf[cols, :], bt16[...])
        factor = jnp.concatenate(
            [jnp.broadcast_to(f_rows[pl.ds(2 * p + half, 1), :], (HP, TOK)) for half in range(2)], axis=0
        )
        grad = attn[cols, :] + factor * spread
        own = grad * xt[cols, :]
        for half in range(2):
            xdx[pl.ds(2 * p + half, 1), :] = jnp.sum(own[half * HP : (half + 1) * HP], axis=0, keepdims=True)
        for i in range(NB):
            ups[i * BLK : (i + 1) * BLK, cols] = grad[:, i * BLK : (i + 1) * BLK].T.astype(BF16)

    def up_send(i):
        there = up_out.at[:, pl.ds(pl.multiple_of(q * COLS, COLS), COLS)]
        return remote(ups.at[i * BLK : (i + 1) * BLK, :], there, u_send.at[i], u_recv.at[q], at(z, i, before))

    for i in range(NB):
        up_send(i).start()

    db_t = jnp.zeros((N, TOK), F32)
    high, low = split(jnp.concatenate([dsf[c * BLK : (c + 1) * BLK, :].T for c in range(NB)], axis=1))
    db_t = mm(high, fx[0]) + mm(low, fx[0]) + mm(high, fx[1])
    for i in range(NB):
        keys = slice(i * BLK, (i + 1) * BLK)
        dbs[i] = mm_split(dp[keys, :], ca[...]) + db_t[:, keys].T

    def sum_send(kind, o):
        peer = lax.rem(q + o, NB)
        src, dst = ((dbs, dbi), (dcs, dci))[kind]
        return remote(src.at[peer], dst.at[q], o_send.at[kind, o], o_recv.at[kind, q], at(z, peer))

    for o in range(1, NB):
        sum_send(0, o).start()
    dbi[q] = dbs[q]

    for k in range(3):

        @pl.when(bit(z, k))
        def _(k=k):
            @pl.loop(1, NZ)
            def _(o):
                peer = lax.rem(z + o, NZ)
                z_wait(ZKK + k, zkf.at[k, head_rows(peer), :], peer)

            @pl.loop(0, NB)
            def _(p):
                cols = pl.ds(pl.multiple_of(p * BLK, BLK), BLK)
                reach = mm_split(zkf[k, cols, :], ct16[...]) * gt[cols, :]
                for half in range(2):
                    h = 2 * p + half
                    row = jnp.sum(reach[half * HP : (half + 1) * HP], axis=0, keepdims=True)
                    wg[3 + k, pl.ds(h, 1), :] = row * e_rows[pl.ds(h, 1), :]

            high, low = split(jnp.concatenate([zkf[k, c * BLK : (c + 1) * BLK, :].T for c in range(NB)], axis=1))
            dct[...] += mm(high, ag[k, 0]) + mm(low, ag[k, 0]) + mm(high, ag[k, 1])

    high, low = split(dp[...])
    dc_t = dct[...] + mm(bt16[...], high) + mm(bt16[...], low)
    for i in range(NB):
        dcs[i] = dc_t[:, i * BLK : (i + 1) * BLK].T
    for o in range(1, NB):
        sum_send(1, o).start()
    dci[q] = dcs[q]

    @pl.loop(1, NZ)
    def _(o):
        peer = lax.rem(z + o, NZ)
        z_wait(DTT, dti.at[peer], peer)

    later = jnp.sum(
        jnp.concatenate([jnp.sum(dti[h], axis=0, keepdims=True) for h in range(HQ)], axis=0), axis=1, keepdims=True
    )
    pieces = []
    for i in range(NB):
        here = slice(i * BLK, (i + 1) * BLK)
        change = -xdx[:, here]
        for level in range(6):
            change = change + lw[i, level] * wg[level, :, here]
            wgs[i, level] = wg[level, :, here]
        pieces.append(change)
    sums = lanes_sum(jnp.concatenate(pieces, axis=0), onward)
    for i in reversed(range(NB)):
        own = sums[i * HQ : (i + 1) * HQ]
        dgs[i] = own + later
        later = later + own[:, :1]

    mine = pl.ds(pl.multiple_of(q * HQ, HQ), HQ)

    def rows_send(kind, o):
        peer = lax.rem(q + o, NB)
        src, dst = (wgs.at[peer], wg_out.at[:, mine, :]) if kind == 2 else (dgs.at[peer], dg_out.at[mine, :])
        return remote(src, dst, o_send.at[kind, o], o_recv.at[kind, q], at(z, peer))

    for o in range(1, NB):
        rows_send(2, o).start()
        rows_send(3, o).start()
    own_wg = pltpu.make_async_copy(wgs.at[q], wg_out.at[:, mine, :], loc.at[7])
    own_dg = pltpu.make_async_copy(dgs.at[q], dg_out.at[mine, :], loc.at[8])
    own_wg.start()
    own_dg.start()

    for kind, landed in ((0, dbi), (1, dci)):
        for o in range(1, NB):
            peer = lax.rem(q + o, NB)
            there = landed.at[peer]
            remote(there, there, o_send.at[kind, o], o_recv.at[kind, peer], at(z, peer)).wait_recv()
    db_out[...] = dbi[0] + dbi[1] + dbi[2] + dbi[3]
    dc_out[...] = dci[0] + dci[1] + dci[2] + dci[3]

    own_wg.wait()
    own_dg.wait()
    for o in range(1, NB):
        peer = lax.rem(q + o, NB)
        theirs = pl.ds(pl.multiple_of(peer * HQ, HQ), HQ)
        for kind, there in ((2, wg_out.at[:, theirs, :]), (3, dg_out.at[theirs, :])):
            remote(there, there, o_send.at[kind, o], o_recv.at[kind, peer], at(z, peer)).wait_recv()
    for i in range(NB):
        there = up_out.at[:, i * COLS : (i + 1) * COLS]
        remote(there, there, u_send.at[i], u_recv.at[i], at(z, i, before)).wait_recv()

    for kind in range(6):
        for o in range(1, NB):
            group_send(kind, o).wait_send()
    for i in range(NB):
        up_send(i).wait_send()
    for o in range(1, NB):
        sum_send(0, o).wait_send()
        sum_send(1, o).wait_send()
        rows_send(2, o).wait_send()
        rows_send(3, o).wait_send()

    @pl.loop(1, NZ)
    def _(o):
        peer = lax.rem(z + o, NZ)
        z_send_one(TOT, o, tot.at[z], tot.at[z]).wait_send()
        z_send_one(STA, o, st.at[head_rows(peer), :], sti.at[z]).wait_send()
        z_send_one(DST, o, dso.at[peer], dsf.at[head_rows(z), :]).wait_send()
        z_send_one(DTT, o, dto.at[peer], dti.at[z]).wait_send()
        for k in range(3):

            @pl.when(bit(z, k))
            def _(k=k):
                z_send_one(DZK + k, o, dz.at[k, head_rows(peer), :], dzi.at[k, z]).wait_send()

            @pl.when(bit(peer, k))
            def _(k=k):
                z_send_one(ZKK + k, o, zko.at[k, peer], zkf.at[k, head_rows(z), :]).wait_send()


def body(inputs, b_proj, c_proj, decay_log, level_weight, out_grad, final_state_grad):
    def vmem(*shape, dtype=F32):
        return pltpu.VMEM(shape, dtype)

    scratch = [
        vmem(TOK, COLS, dtype=BF16),
        vmem(TOK, COLS, dtype=BF16),
        vmem(TOK, N, dtype=BF16),
        vmem(TOK, N, dtype=BF16),
        vmem(NB, HQ, BLK),
        vmem(NB, 6, HQ, BLK),
        vmem(HP, N),
        vmem(COLS, TOK),
        vmem(COLS, TOK),
        vmem(COLS, TOK, dtype=BF16),
        vmem(N, TOK, dtype=BF16),
        vmem(N, TOK, dtype=BF16),
        vmem(HQ, TOK),
        vmem(HQ, TOK),
        vmem(HQ, TOK),
        vmem(3, HQ, TOK),
        vmem(NB, HQ, TOK),
        vmem(3, 2, COLS, TOK, dtype=BF16),
        vmem(2, COLS, TOK, dtype=BF16),
        vmem(TOK, TOK),
        vmem(TOK, TOK),
        vmem(COLS, TOK),
        vmem(TOK, COLS, dtype=BF16),
        vmem(3, COLS, N),
        vmem(COLS, N),
        vmem(NZ, HQ, BLK),
        vmem(3, NZ, HP, N),
        vmem(NZ, HP, N),
        vmem(NZ, HP, N),
        vmem(3, NZ, HP, N),
        vmem(NZ, 8, N),
        vmem(COLS, N),
        vmem(3, COLS, N),
        vmem(NZ, 8, N),
        vmem(6, HQ, TOK),
        vmem(N, TOK),
        vmem(NB, BLK, N),
        vmem(NB, BLK, N),
        vmem(NB, BLK, N),
        vmem(NB, BLK, N),
        vmem(NB, 6, HQ, BLK),
        vmem(NB, HQ, BLK),
        vmem(HQ, TOK),
        pltpu.SemaphoreType.DMA((6, NB)),
        pltpu.SemaphoreType.DMA((6, NB)),
        pltpu.SemaphoreType.DMA((10, NZ)),
        pltpu.SemaphoreType.DMA((10, NZ)),
        pltpu.SemaphoreType.DMA((NB,)),
        pltpu.SemaphoreType.DMA((NB,)),
        pltpu.SemaphoreType.DMA((4, NB)),
        pltpu.SemaphoreType.DMA((4, NB)),
        pltpu.SemaphoreType.DMA((9,)),
    ]
    anywhere = pl.BlockSpec(memory_space=pl.ANY)
    made = (
        jax.ShapeDtypeStruct((BLK, HEADS * HP), BF16),
        jax.ShapeDtypeStruct((BLK, N), F32),
        jax.ShapeDtypeStruct((BLK, N), F32),
        jax.ShapeDtypeStruct((6, HEADS, BLK), F32),
        jax.ShapeDtypeStruct((HEADS, BLK), F32),
    )
    up, db, dc, wg, dg = pl.pallas_call(
        kernel,
        out_shape=made,
        in_specs=[anywhere] * 7,
        out_specs=(anywhere, pl.BlockSpec(memory_space=pltpu.VMEM), pl.BlockSpec(memory_space=pltpu.VMEM), anywhere, anywhere),
        scratch_shapes=scratch,
        compiler_params=pltpu.CompilerParams(
            collective_id=0, has_side_effects=True, vmem_limit_bytes=40 * 2**20
        ),
    )(
        inputs[0],
        out_grad[0],
        b_proj[0],
        c_proj[0],
        decay_log[0].T,
        jnp.transpose(level_weight[0], (1, 2, 0)),
        jnp.transpose(final_state_grad[0], (0, 2, 1)),
    )
    return (up[None], db[None], dc[None], dg.T[None], jnp.transpose(wg, (2, 0, 1))[None])


def solution(mesh):
    rows = P("section", "seq", None)
    deep = P("section", "seq", None, None)
    return jax.shard_map(
        body,
        mesh=mesh,
        in_specs=(rows, rows, rows, rows, deep, rows, P("section", None, None, None)),
        out_specs=(rows, rows, rows, rows, deep),
        check_vma=False,
    )
```

```python
import jax
import jax.numpy as jnp
from jax import lax
from jax.experimental import pallas as pl
from jax.experimental.pallas import tpu as pltpu
from jax.sharding import PartitionSpec as P

MESH = pl.DeviceIdType.MESH
F32, BF16 = jnp.float32, jnp.bfloat16
BLK = 128
NB = 4
NZ = 8
HEADS = 32
HQ = HEADS // NB
HP = 64
N = 128
TOK = NB * BLK
COLS = HQ * HP
SECTIONS = 8
AHEAD = 3
DEC, LWT, CPR, GRD, BPR, INP = range(6)
TOT, DZK, STA, DST, ZKK, DTT = 0, 1, 4, 5, 6, 9


def level_of(low, high):
    return (low ^ high).bit_length() - 1


def split(value):
    high = value.astype(BF16)
    return high, (value - high.astype(F32)).astype(BF16)


def mm(a, b):
    return jnp.dot(a, b, preferred_element_type=F32)


def mm_split(a, b16):
    high, low = split(a)
    return mm(high, b16) + mm(low, b16)


def lanes_sum(value, tri):
    first = value.astype(BF16)
    rest = value - first.astype(F32)
    second = rest.astype(BF16)
    third = (rest - second.astype(F32)).astype(BF16)
    return mm(first, tri) + mm(second, tri) + mm(third, tri)


def kernel(
    x_hbm, g_hbm, b_hbm, c_hbm, dec_hbm, lw_hbm, fsg_hbm,
    up_out, db_out, dc_out, wg_out, dg_out,
    xa, ga, ba, ca, dec, lw, fsg,
    xt, gt, gt16, bt16, ct16,
    r_rows, e_rows, f_rows, a_rows, w_rows,
    ag, fx, sp, dp, attn, ups,
    dz, st, tot, dzi, sti, dso, zko, dto, dsf, zkf, dti,
    wg, dct, dbs, dcs, dbi, dci, wgs, dgs, xdx, near, low_dz,
    a_send, a_recv, z_send, z_recv, n_send, n_recv, u_send, u_recv, o_send, o_recv, loc,
):
    seq = lax.axis_index("seq")
    sec = lax.axis_index("section")
    z = seq // NB
    q = lax.rem(seq, NB)
    before = lax.rem(sec + SECTIONS - 1, SECTIONS)
    after = lax.rem(sec + 1, SECTIONS)

    def at(zz, qq, section=sec):
        return {"seq": zz * NB + qq, "section": section}

    def remote(src, dst, send_sem, recv_sem, where):
        return pltpu.make_async_remote_copy(
            src_ref=src, dst_ref=dst, send_sem=send_sem, recv_sem=recv_sem,
            device_id=where, device_id_type=MESH,
        )

    barrier = pltpu.get_barrier_semaphore()

    def greet(where):
        pl.semaphore_signal(barrier, inc=1, device_id=where, device_id_type=MESH)

    for o in range(1, NB):
        greet(at(z, lax.rem(q + o, NB)))
    for o in range(1, NZ):
        greet(at(lax.rem(z + o, NZ), q))
    for i in range(NB):
        greet(at(z, i, before))
        greet(at(z, i, after))
    pl.semaphore_wait(barrier, NB - 1 + NZ - 1 + 2 * NB)

    def pair_at(j):
        return lax.rem(z // 2 + 1 + j, NB)

    def piece(kind, owner, slot, j):
        heads = pl.ds(pl.multiple_of(owner * HQ, HQ), HQ)
        there = pl.ds(pl.multiple_of(pair_at(j) * BLK, BLK), BLK)
        cols = pl.ds(pl.multiple_of(owner * COLS + pair_at(j) * BLK, BLK), BLK)
        rows = pl.ds(pl.multiple_of(slot * BLK, BLK), BLK)
        if kind == DEC:
            return dec_hbm.at[heads, :], dec.at[slot]
        if kind == LWT:
            return lw_hbm.at[:, heads, :], lw.at[slot]
        if kind == CPR:
            return c_hbm, ca.at[rows, :]
        if kind == GRD:
            return g_hbm.at[:, cols], ga.at[rows, there]
        if kind == BPR:
            return b_hbm, ba.at[rows, :]
        return x_hbm.at[:, cols], xa.at[rows, there]

    def group_send(kind, o, j):
        peer = lax.rem(q + o, NB)
        src, dst = piece(kind, peer, q, j)
        return remote(src, dst, a_send.at[kind, j, o], a_recv.at[kind, j, q], at(z, peer))

    def group_start(kind, j=0):
        for o in range(1, NB):
            group_send(kind, o, j).start()
        src, dst = piece(kind, q, q, j)
        pltpu.make_async_copy(src, dst, loc.at[kind, j]).start()

    def group_wait(kind, j=0):
        src, dst = piece(kind, q, q, j)
        pltpu.make_async_copy(src, dst, loc.at[kind, j]).wait()
        for o in range(1, NB):
            peer = lax.rem(q + o, NB)
            dst = piece(kind, peer, peer, j)[1]
            remote(dst, dst, a_send.at[kind, j, o], a_recv.at[kind, j, peer], at(z, peer)).wait_recv()

    for kind in (DEC, LWT, CPR):
        group_start(kind)
    for j in range(AHEAD):
        group_start(GRD, j)
    final_copy = pltpu.make_async_copy(fsg_hbm.at[q * HQ + z], fsg, loc.at[6, 0])
    final_copy.start()

    row_of = lax.broadcasted_iota(jnp.int32, (BLK, BLK), 0)
    col_of = lax.broadcasted_iota(jnp.int32, (BLK, BLK), 1)
    causal = row_of <= col_of
    upto = jnp.where(causal, 1.0, 0.0).astype(BF16)
    onward = jnp.where(row_of >= col_of, 1.0, 0.0).astype(BF16)
    left = lax.broadcasted_iota(jnp.int32, (BLK, BLK), 1) < HP

    group_wait(DEC)
    running = lanes_sum(jnp.concatenate([dec[i] for i in range(NB)], axis=0), upto)
    sofar = jnp.zeros((HQ, 1), F32)
    for i in range(NB):
        own = running[i * HQ : (i + 1) * HQ]
        r_rows[:, i * BLK : (i + 1) * BLK] = own + sofar
        sofar = sofar + own[:, BLK - 1 : BLK]
    tot[z] = jnp.broadcast_to(sofar, (HQ, BLK))

    def z_send_one(kind, peer, src, dst):
        return remote(src, dst, z_send.at[kind, peer], z_recv.at[kind, z], at(peer, q))

    def z_wait(kind, dst, peer):
        remote(dst, dst, z_send.at[kind, 0], z_recv.at[kind, peer], at(peer, q)).wait_recv()

    @pl.loop(1, NZ)
    def _(o):
        z_send_one(TOT, lax.rem(z + o, NZ), tot.at[z], tot.at[z]).start()

    r_all = r_rows[...]
    e_rows[...] = jnp.exp(r_all)
    f_rows[...] = jnp.exp(sofar - r_all)
    group_wait(LWT)
    for k in range(3):
        for i in range(NB):
            a_rows[k, :, i * BLK : (i + 1) * BLK] = lw[i, 3 + k] * e_rows[:, i * BLK : (i + 1) * BLK]
    for i in range(NB):
        for j in range(i, NB):
            w_rows[i, :, j * BLK : (j + 1) * BLK] = lw[j, level_of(i, j) + 1]

    group_wait(CPR)
    for i in range(NB):
        ct16[:, i * BLK : (i + 1) * BLK] = ca[i * BLK : (i + 1) * BLK, :].astype(F32).T.astype(BF16)
    wg[...] = jnp.zeros_like(wg)
    dct[...] = jnp.zeros_like(dct)
    dp[...] = jnp.zeros_like(dp)

    def bit(zz, k):
        return lax.rem(zz // 2**k, 2) == 1

    def head_rows(h):
        return pl.ds(pl.multiple_of(h * HP, HP), HP)

    def pair_rows(p):
        return pl.ds(pl.multiple_of(p * BLK, BLK), BLK)

    def to_owners(kind, p, source, landing):
        for half in range(2):
            owner = 2 * p + half

            @pl.when(owner != z)
            def _(owner=owner):
                z_send_one(kind, owner, source.at[head_rows(owner), :], landing.at[z]).start()

            @pl.when(owner == z)
            def _(owner=owner):
                landing[z] = source[head_rows(owner), :]

    def down_send(p):
        return remote(dz.at[0, pair_rows(p), :], low_dz.at[pair_rows(p), :], n_send.at[0, p], n_recv.at[0, p], at(z - 1, q))

    def up_state(p):
        return remote(st.at[pair_rows(p), :], zkf.at[0, pair_rows(p), :], n_send.at[1, p], n_recv.at[1, p], at(z + 1, q))

    @pl.loop(0, NB)
    def _(j):
        p = pair_at(j)
        cols = pair_rows(p)
        group_wait(GRD, j)

        @pl.when(j < NB - AHEAD)
        def _():
            group_start(GRD, j + AHEAD)

        @pl.when(j == NB - AHEAD)
        def _():
            group_start(BPR)

        @pl.when(j >= NB - AHEAD)
        def _():
            group_start(INP, j + AHEAD - NB)

        for i in range(NB):
            rows = ga[i * BLK : (i + 1) * BLK, cols].astype(F32).T
            gt[cols, i * BLK : (i + 1) * BLK] = rows
            gt16[cols, i * BLK : (i + 1) * BLK] = rows.astype(BF16)
        for k in range(3):

            @pl.when(bit(z, k))
            def _(k=k):
                for half in range(2):
                    rows = head_rows(2 * p + half)
                    high, low = split(gt[rows, :] * a_rows[k, pl.ds(2 * p + half, 1), :])
                    ag[k, 0, rows, :] = high
                    ag[k, 1, rows, :] = low
                dz[k, cols, :] = mm(ag[k, 0, cols, :], ca[...]) + mm(ag[k, 1, cols, :], ca[...])
                if k == 0:
                    down_send(p).start()
                else:
                    to_owners(DZK + k, p, dz.at[k], dzi.at[k])

    group_wait(BPR)
    for i in range(NB):
        bt16[:, i * BLK : (i + 1) * BLK] = ba[i * BLK : (i + 1) * BLK, :].astype(F32).T.astype(BF16)

    @pl.loop(0, NB)
    def _(j):
        p = pair_at(j)
        cols = pair_rows(p)
        group_wait(INP, j)

        @pl.when(j == 0)
        def _():
            group_start(INP, NB - 1)

        for i in range(NB):
            xt[cols, i * BLK : (i + 1) * BLK] = xa[i * BLK : (i + 1) * BLK, cols].astype(F32).T
        for half in range(2):
            rows = head_rows(2 * p + half)
            high, low = split(xt[rows, :] * f_rows[pl.ds(2 * p + half, 1), :])
            fx[0, rows, :] = high
            fx[1, rows, :] = low
        st[cols, :] = mm(fx[0, cols, :], ba[...]) + mm(fx[1, cols, :], ba[...])

        @pl.when(jnp.logical_not(bit(z, 0)))
        def _():
            up_state(p).start()

        to_owners(STA, p, st, sti)

    @pl.loop(1, NZ)
    def _(o):
        peer = lax.rem(z + o, NZ)
        z_wait(TOT, tot.at[peer], peer)

    for k in range(1, 3):

        @pl.loop(1, NZ)
        def _(o, k=k):
            peer = lax.rem(z + o, NZ)

            @pl.when(bit(peer, k))
            def _():
                z_wait(DZK + k, dzi.at[k, peer], peer)

    final_copy.wait()
    totals = [tot[d, pl.ds(z, 1), :] for d in range(NZ)]
    weight = {}
    for e in range(NZ):
        gap = jnp.zeros((1, BLK), F32)
        for d in range(e + 1, NZ):
            weight[e, d] = jnp.exp(gap)
            gap = gap + totals[d]
        weight[e, NZ] = jnp.exp(gap)
    for e in range(NZ):
        grad = weight[e, NZ] * fsg[...]
        for d in range(e + 1, NZ):
            if level_of(e, d) == 0:
                continue
            grad = grad + weight[e, d] * dzi[level_of(e, d), d]
        dso[e] = grad

    dsf[head_rows(z), :] = dso[z]

    @pl.loop(1, NZ)
    def _(o):
        peer = lax.rem(z + o, NZ)
        z_send_one(DST, peer, dso.at[peer], dsf.at[head_rows(z), :]).start()

    sp[...] = mm(ba[...], ct16[...])

    @pl.loop(0, NB)
    def _(p):
        cols = pl.ds(pl.multiple_of(p * BLK, BLK), BLK)
        runs = [r_rows[pl.ds(2 * p + half, 1), :] for half in range(2)]
        found = [{(level, j): jnp.zeros((1, BLK), F32) for level in range(3) for j in range(NB)} for _ in range(2)]
        for i in range(NB):
            keys = slice(i * BLK, (i + 1) * BLK)
            pair = []
            for half in range(2):
                keep = left if half == 0 else jnp.logical_not(left)
                own = jnp.where(keep, xa[keys, cols].astype(F32), 0.0).astype(BF16)
                run = runs[half]
                weights = w_rows[i, pl.ds(2 * p + half, 1), :]
                r_keys = jnp.broadcast_to(run[:, keys], (BLK, BLK)).T
                grad = jnp.zeros((BLK, BLK), F32)
                for j in range(i, NB):
                    queries = slice(j * BLK, (j + 1) * BLK)
                    product = mm(own, gt16[cols, queries])
                    spread = run[:, queries] - r_keys
                    if i == j:
                        spread = jnp.where(causal, spread, -1e30)
                    decay = jnp.exp(spread)
                    score = sp[keys, queries]
                    level = level_of(i, j) + 1
                    found[half][level, j] += jnp.sum(product * decay * score, axis=0, keepdims=True)
                    decay = decay * weights[:, queries]
                    dp[keys, queries] += product * decay
                    grad = grad + mm_split(score * decay, ga[queries, cols])
                pair.append(grad)
            attn[cols, keys] = jnp.where(left, pair[0], pair[1]).T
        for half in range(2):
            for level in range(3):
                row = jnp.concatenate([found[half][level, j] for j in range(NB)], axis=1)
                wg[level, pl.ds(2 * p + half, 1), :] = row

    @pl.loop(1, NZ)
    def _(o):
        peer = lax.rem(z + o, NZ)
        z_wait(STA, sti.at[peer], peer)

    for d in range(1, NZ):
        for k in range(1, 3):
            if d >> k & 1:
                base = d - d % 2 ** (k + 1)
                carry = jnp.zeros((HP, N), F32)
                for e in range(base, base + 2**k):
                    carry = carry + weight[e, d] * sti[e]
                zko[k, d] = carry

    for k in range(1, 3):

        @pl.when(bit(z, k))
        def _(k=k):
            zkf[k, head_rows(z), :] = zko[k, z]

        @pl.loop(1, NZ)
        def _(o, k=k):
            peer = lax.rem(z + o, NZ)

            @pl.when(bit(peer, k))
            def _():
                z_send_one(ZKK + k, peer, zko.at[k, peer], zkf.at[k, head_rows(z), :]).start()

    def fold(value):
        return sum(value[8 * i : 8 * (i + 1)] for i in range(HP // 8))

    across = [jnp.zeros((8, N), F32) for _ in range(NZ)]
    for e in range(NZ):
        for d in range(e + 1, NZ + 1):
            if d < NZ and level_of(e, d) == 0:
                continue
            other = fsg[...] if d == NZ else dzi[level_of(e, d), d]
            shared = weight[e, d] * fold(sti[e] * other)
            for f in range(e, d):
                across[f] = across[f] + shared
    for f in range(NZ):
        dto[f] = across[f]
    dti[z] = dto[z]

    @pl.loop(1, NZ)
    def _(o):
        peer = lax.rem(z + o, NZ)
        z_send_one(DTT, peer, dto.at[peer], dti.at[z]).start()

    for p in range(NB):

        @pl.when(jnp.logical_not(bit(z, 0)))
        def _(p=p):
            there = low_dz.at[pair_rows(p), :]
            remote(there, there, n_send.at[0, p], n_recv.at[0, p], at(z + 1, q)).wait_recv()

        @pl.when(bit(z, 0))
        def _(p=p):
            low_dz[p * BLK : (p + 1) * BLK, :] = jnp.zeros((BLK, N), F32)

    def upstream_send(p, i):
        there = up_out.at[:, pl.ds(pl.multiple_of(q * COLS + p * BLK, BLK), BLK)]
        here = ups.at[i * BLK : (i + 1) * BLK, pair_rows(p)]
        return remote(here, there, u_send.at[p, i], u_recv.at[p, q], at(z, i, before))

    @pl.loop(0, NB)
    def _(j):
        p = pair_at(j)
        cols = pair_rows(p)
        for half in range(2):
            owner = 2 * p + half

            @pl.when(owner != z)
            def _(owner=owner):
                z_wait(DST, dsf.at[head_rows(owner), :], owner)

        state = dsf[cols, :] + low_dz[cols, :]
        dsf[cols, :] = state
        direct = st[cols, :] * low_dz[cols, :]
        spread = mm_split(state, bt16[...])
        factor = jnp.concatenate(
            [jnp.broadcast_to(f_rows[pl.ds(2 * p + half, 1), :], (HP, TOK)) for half in range(2)], axis=0
        )
        grad = attn[cols, :] + factor * spread
        own = grad * xt[cols, :]
        for half in range(2):
            part = slice(half * HP, (half + 1) * HP)
            xdx[pl.ds(2 * p + half, 1), :] = jnp.sum(own[part], axis=0, keepdims=True)
            near[pl.ds(2 * p + half, 1), :] = jnp.sum(direct[part], axis=0, keepdims=True)
        for i in range(NB):
            ups[i * BLK : (i + 1) * BLK, cols] = grad[:, i * BLK : (i + 1) * BLK].T.astype(BF16)
        for i in range(NB):
            upstream_send(p, i).start()

    db_t = jnp.zeros((N, TOK), F32)
    high, low = split(jnp.concatenate([dsf[c * BLK : (c + 1) * BLK, :].T for c in range(NB)], axis=1))
    db_t = mm(high, fx[0]) + mm(low, fx[0]) + mm(high, fx[1])
    for i in range(NB):
        keys = slice(i * BLK, (i + 1) * BLK)
        dbs[i] = mm_split(dp[keys, :], ca[...]) + db_t[:, keys].T

    def sum_send(kind, o):
        peer = lax.rem(q + o, NB)
        src, dst = ((dbs, dbi), (dcs, dci))[kind]
        return remote(src.at[peer], dst.at[q], o_send.at[kind, o], o_recv.at[kind, q], at(z, peer))

    for o in range(1, NB):
        sum_send(0, o).start()
    dbi[q] = dbs[q]

    for k in range(3):

        @pl.when(bit(z, k))
        def _(k=k):
            if k == 0:
                for p in range(NB):
                    there = zkf.at[0, pair_rows(p), :]
                    remote(there, there, n_send.at[1, p], n_recv.at[1, p], at(z - 1, q)).wait_recv()
            else:

                @pl.loop(1, NZ)
                def _(o):
                    peer = lax.rem(z + o, NZ)
                    z_wait(ZKK + k, zkf.at[k, head_rows(peer), :], peer)

            @pl.loop(0, NB)
            def _(p):
                cols = pl.ds(pl.multiple_of(p * BLK, BLK), BLK)
                reach = mm_split(zkf[k, cols, :], ct16[...]) * gt[cols, :]
                for half in range(2):
                    h = 2 * p + half
                    row = jnp.sum(reach[half * HP : (half + 1) * HP], axis=0, keepdims=True)
                    wg[3 + k, pl.ds(h, 1), :] = row * e_rows[pl.ds(h, 1), :]

            high, low = split(jnp.concatenate([zkf[k, c * BLK : (c + 1) * BLK, :].T for c in range(NB)], axis=1))
            dct[...] += mm(high, ag[k, 0]) + mm(low, ag[k, 0]) + mm(high, ag[k, 1])

    high, low = split(dp[...])
    dc_t = dct[...] + mm(bt16[...], high) + mm(bt16[...], low)
    for i in range(NB):
        dcs[i] = dc_t[:, i * BLK : (i + 1) * BLK].T
    for o in range(1, NB):
        sum_send(1, o).start()
    dci[q] = dcs[q]

    @pl.loop(1, NZ)
    def _(o):
        peer = lax.rem(z + o, NZ)
        z_wait(DTT, dti.at[peer], peer)

    crossing = jnp.concatenate([jnp.sum(dti[h], axis=0, keepdims=True) for h in range(HQ)], axis=0)
    later = jnp.sum(crossing + near[...], axis=1, keepdims=True)
    pieces = []
    for i in range(NB):
        here = slice(i * BLK, (i + 1) * BLK)
        change = -xdx[:, here]
        for level in range(6):
            change = change + lw[i, level] * wg[level, :, here]
            wgs[i, level] = wg[level, :, here]
        pieces.append(change)
    sums = lanes_sum(jnp.concatenate(pieces, axis=0), onward)
    for i in reversed(range(NB)):
        own = sums[i * HQ : (i + 1) * HQ]
        dgs[i] = own + later
        later = later + own[:, :1]

    mine = pl.ds(pl.multiple_of(q * HQ, HQ), HQ)

    def rows_send(kind, o):
        peer = lax.rem(q + o, NB)
        src, dst = (wgs.at[peer], wg_out.at[:, mine, :]) if kind == 2 else (dgs.at[peer], dg_out.at[mine, :])
        return remote(src, dst, o_send.at[kind, o], o_recv.at[kind, q], at(z, peer))

    for o in range(1, NB):
        rows_send(2, o).start()
        rows_send(3, o).start()
    own_wg = pltpu.make_async_copy(wgs.at[q], wg_out.at[:, mine, :], loc.at[6, 1])
    own_dg = pltpu.make_async_copy(dgs.at[q], dg_out.at[mine, :], loc.at[6, 2])
    own_wg.start()
    own_dg.start()

    for kind, landed in ((0, dbi), (1, dci)):
        for o in range(1, NB):
            peer = lax.rem(q + o, NB)
            there = landed.at[peer]
            remote(there, there, o_send.at[kind, o], o_recv.at[kind, peer], at(z, peer)).wait_recv()
    db_out[...] = dbi[0] + dbi[1] + dbi[2] + dbi[3]
    dc_out[...] = dci[0] + dci[1] + dci[2] + dci[3]

    own_wg.wait()
    own_dg.wait()
    for o in range(1, NB):
        peer = lax.rem(q + o, NB)
        theirs = pl.ds(pl.multiple_of(peer * HQ, HQ), HQ)
        for kind, there in ((2, wg_out.at[:, theirs, :]), (3, dg_out.at[theirs, :])):
            remote(there, there, o_send.at[kind, o], o_recv.at[kind, peer], at(z, peer)).wait_recv()
    for i in range(NB):
        for p in range(NB):
            there = up_out.at[:, i * COLS + p * BLK : i * COLS + (p + 1) * BLK]
            remote(there, there, u_send.at[p, i], u_recv.at[p, i], at(z, i, after)).wait_recv()

    for o in range(1, NB):
        for kind in (DEC, LWT, CPR, BPR):
            group_send(kind, o, 0).wait_send()
        for j in range(NB):
            group_send(GRD, o, j).wait_send()
            group_send(INP, o, j).wait_send()
        sum_send(0, o).wait_send()
        sum_send(1, o).wait_send()
        rows_send(2, o).wait_send()
        rows_send(3, o).wait_send()
    for p in range(NB):
        for i in range(NB):
            upstream_send(p, i).wait_send()

        @pl.when(bit(z, 0))
        def _(p=p):
            down_send(p).wait_send()

        @pl.when(jnp.logical_not(bit(z, 0)))
        def _(p=p):
            up_state(p).wait_send()

    @pl.loop(1, NZ)
    def _(o):
        peer = lax.rem(z + o, NZ)
        z_send_one(TOT, peer, tot.at[z], tot.at[z]).wait_send()
        z_send_one(STA, peer, st.at[head_rows(peer), :], sti.at[z]).wait_send()
        z_send_one(DST, peer, dso.at[peer], dsf.at[head_rows(z), :]).wait_send()
        z_send_one(DTT, peer, dto.at[peer], dti.at[z]).wait_send()
        for k in range(1, 3):

            @pl.when(bit(z, k))
            def _(k=k):
                z_send_one(DZK + k, peer, dz.at[k, head_rows(peer), :], dzi.at[k, z]).wait_send()

            @pl.when(bit(peer, k))
            def _(k=k):
                z_send_one(ZKK + k, peer, zko.at[k, peer], zkf.at[k, head_rows(z), :]).wait_send()


def hand_over(*refs):
    sources, targets, held, sem = refs[:5], refs[5:10], refs[10:15], refs[15]
    taken = [pltpu.make_async_copy(src, mid, sem.at[0, i]) for i, (src, mid) in enumerate(zip(sources, held))]
    given = [pltpu.make_async_copy(mid, dst, sem.at[1, i]) for i, (mid, dst) in enumerate(zip(held, targets))]
    for copy in taken:
        copy.start()
    for first, second in zip(taken, given):
        first.wait()
        second.start()
    for copy in given:
        copy.wait()


def body(inputs, b_proj, c_proj, decay_log, level_weight, out_grad, final_state_grad):
    def vmem(*shape, dtype=F32):
        return pltpu.VMEM(shape, dtype)

    scratch = [
        vmem(TOK, COLS, dtype=BF16),
        vmem(TOK, COLS, dtype=BF16),
        vmem(TOK, N, dtype=BF16),
        vmem(TOK, N, dtype=BF16),
        vmem(NB, HQ, BLK),
        vmem(NB, 6, HQ, BLK),
        vmem(HP, N),
        vmem(COLS, TOK),
        vmem(COLS, TOK),
        vmem(COLS, TOK, dtype=BF16),
        vmem(N, TOK, dtype=BF16),
        vmem(N, TOK, dtype=BF16),
        vmem(HQ, TOK),
        vmem(HQ, TOK),
        vmem(HQ, TOK),
        vmem(3, HQ, TOK),
        vmem(NB, HQ, TOK),
        vmem(3, 2, COLS, TOK, dtype=BF16),
        vmem(2, COLS, TOK, dtype=BF16),
        vmem(TOK, TOK),
        vmem(TOK, TOK),
        vmem(COLS, TOK),
        vmem(TOK, COLS, dtype=BF16),
        vmem(3, COLS, N),
        vmem(COLS, N),
        vmem(NZ, HQ, BLK),
        vmem(3, NZ, HP, N),
        vmem(NZ, HP, N),
        vmem(NZ, HP, N),
        vmem(3, NZ, HP, N),
        vmem(NZ, 8, N),
        vmem(COLS, N),
        vmem(3, COLS, N),
        vmem(NZ, 8, N),
        vmem(6, HQ, TOK),
        vmem(N, TOK),
        vmem(NB, BLK, N),
        vmem(NB, BLK, N),
        vmem(NB, BLK, N),
        vmem(NB, BLK, N),
        vmem(NB, 6, HQ, BLK),
        vmem(NB, HQ, BLK),
        vmem(HQ, TOK),
        vmem(HQ, N),
        vmem(COLS, N),
        pltpu.SemaphoreType.DMA((6, NB, NB)),
        pltpu.SemaphoreType.DMA((6, NB, NB)),
        pltpu.SemaphoreType.DMA((10, NZ)),
        pltpu.SemaphoreType.DMA((10, NZ)),
        pltpu.SemaphoreType.DMA((2, NB)),
        pltpu.SemaphoreType.DMA((2, NB)),
        pltpu.SemaphoreType.DMA((NB, NB)),
        pltpu.SemaphoreType.DMA((NB, NB)),
        pltpu.SemaphoreType.DMA((4, NB)),
        pltpu.SemaphoreType.DMA((4, NB)),
        pltpu.SemaphoreType.DMA((7, NB)),
    ]
    anywhere = pl.BlockSpec(memory_space=pl.ANY)
    made = (
        jax.ShapeDtypeStruct((BLK, HEADS * HP), BF16),
        jax.ShapeDtypeStruct((BLK, N), F32),
        jax.ShapeDtypeStruct((BLK, N), F32),
        jax.ShapeDtypeStruct((6, HEADS, BLK), F32),
        jax.ShapeDtypeStruct((HEADS, BLK), F32),
    )
    results = pl.pallas_call(
        kernel,
        out_shape=made,
        in_specs=[anywhere] * 7,
        out_specs=(anywhere, pl.BlockSpec(memory_space=pltpu.VMEM), pl.BlockSpec(memory_space=pltpu.VMEM), anywhere, anywhere),
        scratch_shapes=scratch,
        compiler_params=pltpu.CompilerParams(
            collective_id=0, has_side_effects=True, vmem_limit_bytes=56 * 2**20
        ),
    )(
        inputs[0],
        out_grad[0],
        b_proj[0],
        c_proj[0],
        decay_log[0].T,
        jnp.transpose(level_weight[0], (1, 2, 0)),
        jnp.transpose(final_state_grad[0], (0, 2, 1)),
    )
    up, db, dc, wg, dg = pl.pallas_call(
        hand_over,
        out_shape=made,
        in_specs=[anywhere] * 5,
        out_specs=[anywhere] * 5,
        scratch_shapes=[*(pltpu.VMEM(m.shape, m.dtype) for m in made), pltpu.SemaphoreType.DMA((2, 5))],
        compiler_params=pltpu.CompilerParams(vmem_limit_bytes=56 * 2**20),
    )(*results)
    return (up[None], db[None], dc[None], dg.T[None], jnp.transpose(wg, (2, 0, 1))[None])


def solution(mesh):
    rows = P("section", "seq", None)
    deep = P("section", "seq", None, None)
    return jax.shard_map(
        body,
        mesh=mesh,
        in_specs=(rows, rows, rows, rows, deep, rows, P("section", None, None, None)),
        out_specs=(rows, rows, rows, rows, deep),
        check_vma=False,
    )
```

```python
import jax
import jax.numpy as jnp
from jax import lax
from jax.experimental import pallas as pl
from jax.experimental.pallas import tpu as pltpu
from jax.sharding import PartitionSpec as P

MESH = pl.DeviceIdType.MESH
F32, BF16 = jnp.float32, jnp.bfloat16
BLK = 128
NB = 4
NZ = 8
HEADS = 32
HQ = HEADS // NB
HP = 64
N = 128
TOK = NB * BLK
COLS = HQ * HP
SECTIONS = 8
AHEAD = 3
DEC, LWT, CPR, GRD, BPR, INP = range(6)
TOT, DZK, JNT, DST, ZKK, DTT = range(6)
GRAD2, STATE2, STATE3, STATE3_FAR, GRAD3, JOIN3, JOIN3_FAR = range(7)
TOP = 4


def level_of(low, high):
    return (low ^ high).bit_length() - 1


def split(value):
    high = value.astype(BF16)
    return high, (value - high.astype(F32)).astype(BF16)


def mm(a, b):
    return jnp.dot(a, b, preferred_element_type=F32)


def mm_split(a, b16):
    high, low = split(a)
    return mm(high, b16) + mm(low, b16)


def lanes_sum(value, tri):
    first = value.astype(BF16)
    rest = value - first.astype(F32)
    second = rest.astype(BF16)
    third = (rest - second.astype(F32)).astype(BF16)
    return mm(first, tri) + mm(second, tri) + mm(third, tri)


def kernel(
    x_hbm, g_hbm, b_hbm, c_hbm, dec_hbm, lw_hbm, fsg_hbm,
    up_out, db_out, dc_out, wg_out, dg_out,
    xa, ga, ba, ca, dec, lw, fsg,
    xt, gt, gt16, bt16, ct16,
    r_rows, e_rows, f_rows, a_rows, w_rows,
    ag, fx, sp, dp, attn, ups,
    dz, st, tot, dzi, jnt, dso, zko, dto, dsf, zkf, dti,
    wg, dct, dbs, dcs, dbi, dci, wgs, dgs, xdx, near,
    low2, low3, low4, next3, joined, grad3, last, fin,
    a_send, a_recv, z_send, z_recv, n_send, n_recv, u_send, u_recv, o_send, o_recv, loc,
):
    seq = lax.axis_index("seq")
    sec = lax.axis_index("section")
    z = seq // NB
    q = lax.rem(seq, NB)
    before = lax.rem(sec + SECTIONS - 1, SECTIONS)
    after = lax.rem(sec + 1, SECTIONS)

    def at(zz, qq, section=sec):
        return {"seq": zz * NB + qq, "section": section}

    def remote(src, dst, send_sem, recv_sem, where):
        return pltpu.make_async_remote_copy(
            src_ref=src, dst_ref=dst, send_sem=send_sem, recv_sem=recv_sem,
            device_id=where, device_id_type=MESH,
        )

    barrier = pltpu.get_barrier_semaphore()

    def greet(where):
        pl.semaphore_signal(barrier, inc=1, device_id=where, device_id_type=MESH)

    for o in range(1, NB):
        greet(at(z, lax.rem(q + o, NB)))
    for o in range(1, NZ):
        greet(at(lax.rem(z + o, NZ), q))
    for i in range(NB):
        greet(at(z, i, before))
        greet(at(z, i, after))
    pl.semaphore_wait(barrier, NB - 1 + NZ - 1 + 2 * NB)

    def pair_at(j):
        return lax.rem(z // 2 + 1 + j, NB)

    def piece(kind, owner, slot, j):
        heads = pl.ds(pl.multiple_of(owner * HQ, HQ), HQ)
        pair = pair_at(j) if kind == GRD else j
        there = pl.ds(pl.multiple_of(pair * BLK, BLK), BLK)
        cols = pl.ds(pl.multiple_of(owner * COLS + pair * BLK, BLK), BLK)
        rows = pl.ds(pl.multiple_of(slot * BLK, BLK), BLK)
        if kind == DEC:
            return dec_hbm.at[heads, :], dec.at[slot]
        if kind == LWT:
            return lw_hbm.at[:, heads, :], lw.at[slot]
        if kind == CPR:
            return c_hbm, ca.at[rows, :]
        if kind == GRD:
            return g_hbm.at[:, cols], ga.at[rows, there]
        if kind == BPR:
            return b_hbm, ba.at[rows, :]
        return x_hbm.at[:, cols], xa.at[rows, there]

    def group_send(kind, o, j):
        peer = lax.rem(q + o, NB)
        src, dst = piece(kind, peer, q, j)
        return remote(src, dst, a_send.at[kind, j, o], a_recv.at[kind, j, q], at(z, peer))

    def group_start(kind, j=0):
        for o in range(1, NB):
            group_send(kind, o, j).start()
        src, dst = piece(kind, q, q, j)
        pltpu.make_async_copy(src, dst, loc.at[kind, j]).start()

    def group_wait(kind, j=0):
        src, dst = piece(kind, q, q, j)
        pltpu.make_async_copy(src, dst, loc.at[kind, j]).wait()
        for o in range(1, NB):
            peer = lax.rem(q + o, NB)
            dst = piece(kind, peer, peer, j)[1]
            remote(dst, dst, a_send.at[kind, j, o], a_recv.at[kind, j, peer], at(z, peer)).wait_recv()

    for kind in (DEC, BPR):
        group_start(kind)
    for j in range(AHEAD):
        group_start(INP, j)
    final_copy = pltpu.make_async_copy(fsg_hbm.at[pl.ds(pl.multiple_of(q * HQ, HQ), HQ)], fsg, loc.at[6, 0])
    final_copy.start()

    row_of = lax.broadcasted_iota(jnp.int32, (BLK, BLK), 0)
    col_of = lax.broadcasted_iota(jnp.int32, (BLK, BLK), 1)
    causal = row_of <= col_of
    upto = jnp.where(causal, 1.0, 0.0).astype(BF16)
    onward = jnp.where(row_of >= col_of, 1.0, 0.0).astype(BF16)
    left = lax.broadcasted_iota(jnp.int32, (BLK, BLK), 1) < HP

    group_wait(DEC)
    running = lanes_sum(jnp.concatenate([dec[i] for i in range(NB)], axis=0), upto)
    sofar = jnp.zeros((HQ, 1), F32)
    for i in range(NB):
        own = running[i * HQ : (i + 1) * HQ]
        r_rows[:, i * BLK : (i + 1) * BLK] = own + sofar
        sofar = sofar + own[:, BLK - 1 : BLK]
    tot[z] = jnp.broadcast_to(sofar, (HQ, BLK))

    def z_send_one(kind, peer, src, dst):
        return remote(src, dst, z_send.at[kind, peer], z_recv.at[kind, z], at(peer, q))

    def z_wait(kind, dst, peer):
        remote(dst, dst, z_send.at[kind, 0], z_recv.at[kind, peer], at(peer, q)).wait_recv()

    @pl.loop(1, NZ)
    def _(o):
        z_send_one(TOT, lax.rem(z + o, NZ), tot.at[z], tot.at[z]).start()

    r_all = r_rows[...]
    e_rows[...] = jnp.exp(r_all)
    f_rows[...] = jnp.exp(sofar - r_all)
    def bit(zz, k):
        return lax.rem(zz // 2**k, 2) == 1

    def head_rows(h):
        return pl.ds(pl.multiple_of(h * HP, HP), HP)

    def pair_rows(p):
        return pl.ds(pl.multiple_of(p * BLK, BLK), BLK)

    def to_owners(kind, p, source, landing):
        for half in range(2):
            owner = 2 * p + half

            @pl.when(owner != z)
            def _(owner=owner):
                z_send_one(kind, owner, source.at[head_rows(owner), :], landing.at[z]).start()

            @pl.when(owner == z)
            def _(owner=owner):
                landing[z] = source[head_rows(owner), :]

    routes = {
        STATE2: (st, zkf.at[0], 1),
        STATE3: (joined.at[0], zkf.at[1], 1),
        STATE3_FAR: (joined.at[1], zkf.at[1], 2),
        GRAD2: (dz.at[0], low2, -1),
        GRAD3: (dz.at[1], next3, -1),
        JOIN3: (grad3.at[0], low3, -1),
        JOIN3_FAR: (grad3.at[1], low3, -2),
    }

    def near_send(kind, p):
        src, dst, way = routes[kind]
        rows = pair_rows(p)
        return remote(src.at[rows, :], dst.at[rows, :], n_send.at[kind, p], n_recv.at[kind, p], at(z + way, q))

    def near_wait(kind, p):
        _, dst, way = routes[kind]
        there = dst.at[pair_rows(p), :]
        remote(there, there, n_send.at[kind, p], n_recv.at[kind, p], at(z - way, q)).wait_recv()

    def per_pair(rows):
        return jnp.concatenate(
            [jnp.broadcast_to(rows[half : half + 1], (HP, N)) for half in range(2)], axis=0
        )

    def total_of(zz, p):
        return jnp.concatenate([tot[zz, pl.ds(2 * p + half, 1), :] for half in range(2)], axis=0)

    even = jnp.logical_not(bit(z, 0))
    third = lax.rem(z, 4)

    for k in range(3):

        @pl.when(jnp.logical_not(bit(z, k)))
        def _(k=k):
            zkf[k] = jnp.zeros((COLS, N), F32)

    @pl.when(bit(z, 0))
    def _():
        low2[...] = jnp.zeros((COLS, N), F32)

    @pl.when(bit(z, 1))
    def _():
        low3[...] = jnp.zeros((COLS, N), F32)

    @pl.when(bit(z, 2))
    def _():
        low4[...] = jnp.zeros((COLS, N), F32)

    @pl.when(third != 2)
    def _():
        next3[...] = jnp.zeros((COLS, N), F32)

    @pl.when(jnp.logical_or(z < TOP, z == NZ - 1))
    def _():
        dti[...] = jnp.zeros((NZ, 8, N), F32)

    group_wait(BPR)
    for i in range(NB):
        bt16[:, i * BLK : (i + 1) * BLK] = ba[i * BLK : (i + 1) * BLK, :].astype(F32).T.astype(BF16)

    @pl.loop(0, NB)
    def _(p):
        cols = pair_rows(p)
        group_wait(INP, p)

        @pl.when(p < NB - AHEAD)
        def _():
            group_start(INP, p + AHEAD)
            group_start(LWT)
            group_start(CPR)

        @pl.when(p >= NB - AHEAD)
        def _():
            group_start(GRD, p + AHEAD - NB)

        for i in range(NB):
            xt[cols, i * BLK : (i + 1) * BLK] = xa[i * BLK : (i + 1) * BLK, cols].astype(F32).T
        for half in range(2):
            rows = head_rows(2 * p + half)
            high, low = split(xt[rows, :] * f_rows[pl.ds(2 * p + half, 1), :])
            fx[0, rows, :] = high
            fx[1, rows, :] = low
        st[cols, :] = mm(fx[0, cols, :], ba[...]) + mm(fx[1, cols, :], ba[...])

        @pl.when(even)
        def _():
            near_send(STATE2, p).start()

    @pl.loop(1, NZ)
    def _(o):
        peer = lax.rem(z + o, NZ)
        z_wait(TOT, tot.at[peer], peer)

    @pl.when(third == 1)
    def _():
        @pl.loop(0, NB)
        def _(p):
            rows = pair_rows(p)
            near_wait(STATE2, p)
            both = per_pair(jnp.exp(total_of(z, p))) * zkf[0, rows, :] + st[rows, :]
            joined[0, rows, :] = both
            joined[1, rows, :] = per_pair(jnp.exp(total_of(z + 1, p))) * both
            near_send(STATE3, p).start()
            near_send(STATE3_FAR, p).start()

    group_wait(LWT)
    for k in range(3):
        for i in range(NB):
            a_rows[k, :, i * BLK : (i + 1) * BLK] = lw[i, 3 + k] * e_rows[:, i * BLK : (i + 1) * BLK]
    for i in range(NB):
        for j in range(i, NB):
            w_rows[i, :, j * BLK : (j + 1) * BLK] = lw[j, level_of(i, j) + 1]

    group_wait(CPR)
    for i in range(NB):
        ct16[:, i * BLK : (i + 1) * BLK] = ca[i * BLK : (i + 1) * BLK, :].astype(F32).T.astype(BF16)
    wg[...] = jnp.zeros_like(wg)
    dct[...] = jnp.zeros_like(dct)
    dp[...] = jnp.zeros_like(dp)

    @pl.loop(0, NB)
    def _(j):
        p = pair_at(j)
        cols = pair_rows(p)
        group_wait(GRD, j)

        @pl.when(j < NB - AHEAD)
        def _():
            group_start(GRD, j + AHEAD)

        for i in range(NB):
            rows = ga[i * BLK : (i + 1) * BLK, cols].astype(F32).T
            gt[cols, i * BLK : (i + 1) * BLK] = rows
            gt16[cols, i * BLK : (i + 1) * BLK] = rows.astype(BF16)
        for k in (2, 1, 0):

            @pl.when(bit(z, k))
            def _(k=k):
                for half in range(2):
                    rows = head_rows(2 * p + half)
                    high, low = split(gt[rows, :] * a_rows[k, pl.ds(2 * p + half, 1), :])
                    ag[k, 0, rows, :] = high
                    ag[k, 1, rows, :] = low
                dz[k, cols, :] = mm(ag[k, 0, cols, :], ca[...]) + mm(ag[k, 1, cols, :], ca[...])
                if k == 2:
                    to_owners(DZK, p, dz.at[k], dzi)
                elif k == 1:

                    @pl.when(third == 3)
                    def _():
                        near_send(GRAD3, p).start()
                else:
                    near_send(GRAD2, p).start()

    @pl.when(z == TOP - 1)
    def _():
        @pl.loop(0, NB)
        def _(p):
            rows = pair_rows(p)
            near_wait(STATE2, p)
            near_wait(STATE3_FAR, p)
            carried = zkf[0, rows, :] + zkf[1, rows, :]
            joined[0, rows, :] = per_pair(jnp.exp(total_of(z, p))) * carried + st[rows, :]
            to_owners(JNT, p, joined.at[0], jnt)

    @pl.when(third == 2)
    def _():
        @pl.loop(0, NB)
        def _(p):
            rows = pair_rows(p)
            near_wait(GRAD3, p)
            both = dz[1, rows, :] + per_pair(jnp.exp(total_of(z, p))) * next3[rows, :]
            grad3[0, rows, :] = both
            grad3[1, rows, :] = per_pair(jnp.exp(total_of(z - 1, p))) * both
            near_send(JOIN3, p).start()
            near_send(JOIN3_FAR, p).start()

    sp[...] = mm(ba[...], ct16[...])

    @pl.loop(0, NB)
    def _(p):
        cols = pl.ds(pl.multiple_of(p * BLK, BLK), BLK)
        runs = [r_rows[pl.ds(2 * p + half, 1), :] for half in range(2)]
        found = [{(level, j): jnp.zeros((1, BLK), F32) for level in range(3) for j in range(NB)} for _ in range(2)]
        for i in range(NB):
            keys = slice(i * BLK, (i + 1) * BLK)
            pair = []
            for half in range(2):
                keep = left if half == 0 else jnp.logical_not(left)
                own = jnp.where(keep, xa[keys, cols].astype(F32), 0.0).astype(BF16)
                run = runs[half]
                weights = w_rows[i, pl.ds(2 * p + half, 1), :]
                r_keys = jnp.broadcast_to(run[:, keys], (BLK, BLK)).T
                grad = jnp.zeros((BLK, BLK), F32)
                for j in range(i, NB):
                    queries = slice(j * BLK, (j + 1) * BLK)
                    product = mm(own, gt16[cols, queries])
                    spread = run[:, queries] - r_keys
                    if i == j:
                        spread = jnp.where(causal, spread, -1e30)
                    decay = jnp.exp(spread)
                    score = sp[keys, queries]
                    level = level_of(i, j) + 1
                    found[half][level, j] += jnp.sum(product * decay * score, axis=0, keepdims=True)
                    decay = decay * weights[:, queries]
                    dp[keys, queries] += product * decay
                    grad = grad + mm_split(score * decay, ga[queries, cols])
                pair.append(grad)
            attn[cols, keys] = jnp.where(left, pair[0], pair[1]).T
        for half in range(2):
            for level in range(3):
                row = jnp.concatenate([found[half][level, j] for j in range(NB)], axis=1)
                wg[level, pl.ds(2 * p + half, 1), :] = row

    for d in range(TOP, NZ):

        @pl.when(z != d)
        def _(d=d):
            z_wait(DZK, dzi.at[d], d)

    totals = [tot[d, pl.ds(z, 1), :] for d in range(NZ)]
    upto_here = {TOP: jnp.zeros((1, N), F32)}
    for d in range(TOP + 1, NZ):
        upto_here[d] = upto_here[d - 1] + totals[d - 1]
    reach4 = {d: jnp.exp(gap) for d, gap in upto_here.items()}
    joint_grad = dzi[TOP]
    for d in range(TOP + 1, NZ):
        joint_grad = joint_grad + reach4[d] * dzi[d]
    gap = jnp.zeros((1, N), F32)
    for e in reversed(range(TOP)):
        dso[e] = jnp.exp(gap) * joint_grad
        gap = gap + totals[e]

        @pl.when(z != e)
        def _(e=e):
            z_send_one(DST, e, dso.at[e], low4.at[head_rows(z), :]).start()

        @pl.when(z == e)
        def _(e=e):
            low4[head_rows(z), :] = dso[e]

    @pl.when(z != TOP - 1)
    def _():
        z_wait(JNT, jnt.at[TOP - 1], TOP - 1)

    for d in range(TOP, NZ):
        zko[d] = reach4[d] * jnt[TOP - 1]

        @pl.when(z != d)
        def _(d=d):
            z_send_one(ZKK, d, zko.at[d], zkf.at[2, head_rows(z), :]).start()

        @pl.when(z == d)
        def _(d=d):
            zkf[2, head_rows(z), :] = zko[d]

    def fold(value):
        return sum(value[8 * i : 8 * (i + 1)] for i in range(HP // 8))

    across = jnp.zeros((8, N), F32)
    for f in reversed(range(TOP, NZ - 1)):
        across = across + fold(zko[f + 1] * dzi[f + 1])
        dto[f] = across

        @pl.when(z != f)
        def _(f=f):
            z_send_one(DTT, f, dto.at[f], dti.at[z]).start()

        @pl.when(z == f)
        def _(f=f):
            dti[z] = dto[f]

    final_copy.wait()
    rest = jnp.zeros((HQ, N), F32)
    for f in range(1, NZ):
        rest = rest + tot[f] * jnp.where(z < f, 1.0, 0.0)
    fin[...] = jnp.exp(rest)

    def upstream_send(p, i):
        there = up_out.at[:, pl.ds(pl.multiple_of(q * COLS + p * BLK, BLK), BLK)]
        here = ups.at[i * BLK : (i + 1) * BLK, pair_rows(p)]
        return remote(here, there, u_send.at[p, i], u_recv.at[p, q], at(z, i, before))

    @pl.loop(0, NB)
    def _(j):
        p = pair_at(j)
        cols = pair_rows(p)

        @pl.when(even)
        def _():
            near_wait(GRAD2, p)

        @pl.when(third == 1)
        def _():
            near_wait(JOIN3, p)

        @pl.when(third == 0)
        def _():
            near_wait(JOIN3_FAR, p)

        for half in range(2):
            owner = 2 * p + half

            @pl.when(jnp.logical_and(z < TOP, owner != z))
            def _(owner=owner):
                z_wait(DST, low4.at[head_rows(owner), :], owner)

        weight = jnp.concatenate([fin[pl.ds(2 * p + half, 1), :] for half in range(2)], axis=0)
        ending = per_pair(weight) * fsg[pl.ds(2 * p, 2)].reshape(BLK, N)
        last[cols, :] = ending
        state = ending + low2[cols, :] + low3[cols, :] + low4[cols, :]
        dsf[cols, :] = state
        spread = mm_split(state, bt16[...])
        factor = jnp.concatenate(
            [jnp.broadcast_to(f_rows[pl.ds(2 * p + half, 1), :], (HP, TOK)) for half in range(2)], axis=0
        )
        grad = attn[cols, :] + factor * spread
        own = grad * xt[cols, :]
        for half in range(2):
            part = slice(half * HP, (half + 1) * HP)
            xdx[pl.ds(2 * p + half, 1), :] = jnp.sum(own[part], axis=0, keepdims=True)
        for i in range(NB):
            ups[i * BLK : (i + 1) * BLK, cols] = grad[:, i * BLK : (i + 1) * BLK].T.astype(BF16)
        for i in range(NB):
            upstream_send(p, i).start()

    db_t = jnp.zeros((N, TOK), F32)
    high, low = split(jnp.concatenate([dsf[c * BLK : (c + 1) * BLK, :].T for c in range(NB)], axis=1))
    db_t = mm(high, fx[0]) + mm(low, fx[0]) + mm(high, fx[1])
    for i in range(NB):
        keys = slice(i * BLK, (i + 1) * BLK)
        dbs[i] = mm_split(dp[keys, :], ca[...]) + db_t[:, keys].T

    def sum_send(kind, o):
        peer = lax.rem(q + o, NB)
        src, dst = ((dbs, dbi), (dcs, dci))[kind]
        return remote(src.at[peer], dst.at[q], o_send.at[kind, o], o_recv.at[kind, q], at(z, peer))

    for o in range(1, NB):
        sum_send(0, o).start()
    dbi[q] = dbs[q]

    for k in range(3):

        @pl.when(bit(z, k))
        def _(k=k):
            if k == 0:

                @pl.when(z == NZ - 1)
                def _():
                    for p in range(NB):
                        near_wait(STATE2, p)
            elif k == 1:

                @pl.when(third == 2)
                def _():
                    for p in range(NB):
                        near_wait(STATE3, p)

                @pl.when(z == NZ - 1)
                def _():
                    for p in range(NB):
                        near_wait(STATE3_FAR, p)
            else:

                @pl.loop(1, NZ)
                def _(o):
                    peer = lax.rem(z + o, NZ)
                    z_wait(ZKK, zkf.at[2, head_rows(peer), :], peer)

            @pl.loop(0, NB)
            def _(p):
                cols = pl.ds(pl.multiple_of(p * BLK, BLK), BLK)
                reach = mm_split(zkf[k, cols, :], ct16[...]) * gt[cols, :]
                for half in range(2):
                    h = 2 * p + half
                    row = jnp.sum(reach[half * HP : (half + 1) * HP], axis=0, keepdims=True)
                    wg[3 + k, pl.ds(h, 1), :] = row * e_rows[pl.ds(h, 1), :]

            high, low = split(jnp.concatenate([zkf[k, c * BLK : (c + 1) * BLK, :].T for c in range(NB)], axis=1))
            dct[...] += mm(high, ag[k, 0]) + mm(low, ag[k, 0]) + mm(high, ag[k, 1])

    high, low = split(dp[...])
    dc_t = dct[...] + mm(bt16[...], high) + mm(bt16[...], low)
    for i in range(NB):
        dcs[i] = dc_t[:, i * BLK : (i + 1) * BLK].T
    for o in range(1, NB):
        sum_send(1, o).start()
    dci[q] = dcs[q]

    @pl.when(jnp.logical_and(z >= TOP, z < NZ - 1))
    def _():
        @pl.loop(1, NZ)
        def _(o):
            peer = lax.rem(z + o, NZ)
            z_wait(DTT, dti.at[peer], peer)

    @pl.loop(0, NB)
    def _(p):
        rows = pair_rows(p)
        lower = zkf[0, rows, :] + zkf[1, rows, :]
        carried = zkf[1, rows, :] * next3[rows, :] + zkf[0, rows, :] * low3[rows, :]
        carried = carried + lower * low4[rows, :] + (lower + zkf[2, rows, :]) * last[rows, :]
        own = st[rows, :] * dsf[rows, :] + per_pair(jnp.exp(total_of(z, p))) * carried
        for half in range(2):
            part = slice(half * HP, (half + 1) * HP)
            near[pl.ds(2 * p + half, 1), :] = jnp.sum(own[part], axis=0, keepdims=True)

    crossing = jnp.concatenate([jnp.sum(dti[h], axis=0, keepdims=True) for h in range(HQ)], axis=0)
    later = jnp.sum(crossing + near[...], axis=1, keepdims=True)
    pieces = []
    for i in range(NB):
        here = slice(i * BLK, (i + 1) * BLK)
        change = -xdx[:, here]
        for level in range(6):
            change = change + lw[i, level] * wg[level, :, here]
            wgs[i, level] = wg[level, :, here]
        pieces.append(change)
    sums = lanes_sum(jnp.concatenate(pieces, axis=0), onward)
    for i in reversed(range(NB)):
        own = sums[i * HQ : (i + 1) * HQ]
        dgs[i] = own + later
        later = later + own[:, :1]

    mine = pl.ds(pl.multiple_of(q * HQ, HQ), HQ)

    def rows_send(kind, o):
        peer = lax.rem(q + o, NB)
        src, dst = (wgs.at[peer], wg_out.at[:, mine, :]) if kind == 2 else (dgs.at[peer], dg_out.at[mine, :])
        return remote(src, dst, o_send.at[kind, o], o_recv.at[kind, q], at(z, peer))

    for o in range(1, NB):
        rows_send(2, o).start()
        rows_send(3, o).start()
    own_wg = pltpu.make_async_copy(wgs.at[q], wg_out.at[:, mine, :], loc.at[6, 1])
    own_dg = pltpu.make_async_copy(dgs.at[q], dg_out.at[mine, :], loc.at[6, 2])
    own_wg.start()
    own_dg.start()

    for kind, landed in ((0, dbi), (1, dci)):
        for o in range(1, NB):
            peer = lax.rem(q + o, NB)
            there = landed.at[peer]
            remote(there, there, o_send.at[kind, o], o_recv.at[kind, peer], at(z, peer)).wait_recv()
    db_out[...] = dbi[0] + dbi[1] + dbi[2] + dbi[3]
    dc_out[...] = dci[0] + dci[1] + dci[2] + dci[3]

    own_wg.wait()
    own_dg.wait()
    for o in range(1, NB):
        peer = lax.rem(q + o, NB)
        theirs = pl.ds(pl.multiple_of(peer * HQ, HQ), HQ)
        for kind, there in ((2, wg_out.at[:, theirs, :]), (3, dg_out.at[theirs, :])):
            remote(there, there, o_send.at[kind, o], o_recv.at[kind, peer], at(z, peer)).wait_recv()
    for i in range(NB):
        for p in range(NB):
            there = up_out.at[:, i * COLS + p * BLK : i * COLS + (p + 1) * BLK]
            remote(there, there, u_send.at[p, i], u_recv.at[p, i], at(z, i, after)).wait_recv()

    for o in range(1, NB):
        for kind in (DEC, LWT, CPR, BPR):
            group_send(kind, o, 0).wait_send()
        for j in range(NB):
            group_send(GRD, o, j).wait_send()
            group_send(INP, o, j).wait_send()
        sum_send(0, o).wait_send()
        sum_send(1, o).wait_send()
        rows_send(2, o).wait_send()
        rows_send(3, o).wait_send()
    for p in range(NB):
        for i in range(NB):
            upstream_send(p, i).wait_send()

        @pl.when(even)
        def _(p=p):
            near_send(STATE2, p).wait_send()

        @pl.when(bit(z, 0))
        def _(p=p):
            near_send(GRAD2, p).wait_send()

        @pl.when(third == 1)
        def _(p=p):
            near_send(STATE3, p).wait_send()
            near_send(STATE3_FAR, p).wait_send()

        @pl.when(third == 2)
        def _(p=p):
            near_send(JOIN3, p).wait_send()
            near_send(JOIN3_FAR, p).wait_send()

        @pl.when(third == 3)
        def _(p=p):
            near_send(GRAD3, p).wait_send()

    @pl.loop(1, NZ)
    def _(o):
        peer = lax.rem(z + o, NZ)
        z_send_one(TOT, peer, tot.at[z], tot.at[z]).wait_send()

        @pl.when(z >= TOP)
        def _():
            z_send_one(DZK, peer, dz.at[2, head_rows(peer), :], dzi.at[z]).wait_send()

        @pl.when(z == TOP - 1)
        def _():
            z_send_one(JNT, peer, joined.at[0, head_rows(peer), :], jnt.at[z]).wait_send()

        @pl.when(peer < TOP)
        def _():
            z_send_one(DST, peer, dso.at[peer], low4.at[head_rows(z), :]).wait_send()

        @pl.when(peer >= TOP)
        def _():
            z_send_one(ZKK, peer, zko.at[peer], zkf.at[2, head_rows(z), :]).wait_send()

        @pl.when(jnp.logical_and(peer >= TOP, peer < NZ - 1))
        def _():
            z_send_one(DTT, peer, dto.at[peer], dti.at[z]).wait_send()


def hand_over(*refs):
    sources, targets, held, sem = refs[:5], refs[5:10], refs[10:15], refs[15]
    taken = [pltpu.make_async_copy(src, mid, sem.at[0, i]) for i, (src, mid) in enumerate(zip(sources, held))]
    given = [pltpu.make_async_copy(mid, dst, sem.at[1, i]) for i, (mid, dst) in enumerate(zip(held, targets))]
    for copy in taken:
        copy.start()
    for first, second in zip(taken, given):
        first.wait()
        second.start()
    for copy in given:
        copy.wait()


def body(inputs, b_proj, c_proj, decay_log, level_weight, out_grad, final_state_grad):
    def vmem(*shape, dtype=F32):
        return pltpu.VMEM(shape, dtype)

    scratch = [
        vmem(TOK, COLS, dtype=BF16),
        vmem(TOK, COLS, dtype=BF16),
        vmem(TOK, N, dtype=BF16),
        vmem(TOK, N, dtype=BF16),
        vmem(NB, HQ, BLK),
        vmem(NB, 6, HQ, BLK),
        vmem(HQ, HP, N),
        vmem(COLS, TOK),
        vmem(COLS, TOK),
        vmem(COLS, TOK, dtype=BF16),
        vmem(N, TOK, dtype=BF16),
        vmem(N, TOK, dtype=BF16),
        vmem(HQ, TOK),
        vmem(HQ, TOK),
        vmem(HQ, TOK),
        vmem(3, HQ, TOK),
        vmem(NB, HQ, TOK),
        vmem(3, 2, COLS, TOK, dtype=BF16),
        vmem(2, COLS, TOK, dtype=BF16),
        vmem(TOK, TOK),
        vmem(TOK, TOK),
        vmem(COLS, TOK),
        vmem(TOK, COLS, dtype=BF16),
        vmem(3, COLS, N),
        vmem(COLS, N),
        vmem(NZ, HQ, BLK),
        vmem(NZ, HP, N),
        vmem(NZ, HP, N),
        vmem(NZ, HP, N),
        vmem(NZ, HP, N),
        vmem(NZ, 8, N),
        vmem(COLS, N),
        vmem(3, COLS, N),
        vmem(NZ, 8, N),
        vmem(6, HQ, TOK),
        vmem(N, TOK),
        vmem(NB, BLK, N),
        vmem(NB, BLK, N),
        vmem(NB, BLK, N),
        vmem(NB, BLK, N),
        vmem(NB, 6, HQ, BLK),
        vmem(NB, HQ, BLK),
        vmem(HQ, TOK),
        vmem(HQ, N),
        vmem(COLS, N),
        vmem(COLS, N),
        vmem(COLS, N),
        vmem(COLS, N),
        vmem(2, COLS, N),
        vmem(2, COLS, N),
        vmem(COLS, N),
        vmem(HQ, N),
        pltpu.SemaphoreType.DMA((6, NB, NB)),
        pltpu.SemaphoreType.DMA((6, NB, NB)),
        pltpu.SemaphoreType.DMA((6, NZ)),
        pltpu.SemaphoreType.DMA((6, NZ)),
        pltpu.SemaphoreType.DMA((7, NB)),
        pltpu.SemaphoreType.DMA((7, NB)),
        pltpu.SemaphoreType.DMA((NB, NB)),
        pltpu.SemaphoreType.DMA((NB, NB)),
        pltpu.SemaphoreType.DMA((4, NB)),
        pltpu.SemaphoreType.DMA((4, NB)),
        pltpu.SemaphoreType.DMA((7, NB)),
    ]
    anywhere = pl.BlockSpec(memory_space=pl.ANY)
    made = (
        jax.ShapeDtypeStruct((BLK, HEADS * HP), BF16),
        jax.ShapeDtypeStruct((BLK, N), F32),
        jax.ShapeDtypeStruct((BLK, N), F32),
        jax.ShapeDtypeStruct((6, HEADS, BLK), F32),
        jax.ShapeDtypeStruct((HEADS, BLK), F32),
    )
    results = pl.pallas_call(
        kernel,
        out_shape=made,
        in_specs=[anywhere] * 7,
        out_specs=(anywhere, pl.BlockSpec(memory_space=pltpu.VMEM), pl.BlockSpec(memory_space=pltpu.VMEM), anywhere, anywhere),
        scratch_shapes=scratch,
        compiler_params=pltpu.CompilerParams(
            collective_id=0, has_side_effects=True, vmem_limit_bytes=56 * 2**20
        ),
    )(
        inputs[0],
        out_grad[0],
        b_proj[0],
        c_proj[0],
        decay_log[0].T,
        jnp.transpose(level_weight[0], (1, 2, 0)),
        jnp.transpose(final_state_grad[0], (0, 2, 1)),
    )
    up, db, dc, wg, dg = pl.pallas_call(
        hand_over,
        out_shape=made,
        in_specs=[anywhere] * 5,
        out_specs=[anywhere] * 5,
        scratch_shapes=[*(pltpu.VMEM(m.shape, m.dtype) for m in made), pltpu.SemaphoreType.DMA((2, 5))],
        compiler_params=pltpu.CompilerParams(vmem_limit_bytes=56 * 2**20),
    )(*results)
    return (up[None], db[None], dc[None], dg.T[None], jnp.transpose(wg, (2, 0, 1))[None])


def solution(mesh):
    rows = P("section", "seq", None)
    deep = P("section", "seq", None, None)
    return jax.shard_map(
        body,
        mesh=mesh,
        in_specs=(rows, rows, rows, rows, deep, rows, P("section", None, None, None)),
        out_specs=(rows, rows, rows, rows, deep),
        check_vma=False,
    )
```

```python
import jax
import jax.numpy as jnp
from jax import lax
from jax.experimental import pallas as pl
from jax.experimental.pallas import tpu as pltpu
from jax.sharding import PartitionSpec as P

MESH = pl.DeviceIdType.MESH
F32, BF16 = jnp.float32, jnp.bfloat16
BLK = 128
NB = 4
NZ = 8
HEADS = 32
HQ = HEADS // NB
HP = 64
N = 128
TOK = NB * BLK
COLS = HQ * HP
SECTIONS = 8
AHEAD = 4
FED = 6
DEC, LWT, CPR, GRD, BPR, INP = range(6)
TOT, DZK, STA, DST, ZKK, DTT = 0, 1, 4, 5, 6, 9


def level_of(low, high):
    return (low ^ high).bit_length() - 1


def split(value):
    high = value.astype(BF16)
    return high, (value - high.astype(F32)).astype(BF16)


def mm(a, b):
    return jnp.dot(a, b, preferred_element_type=F32)


def mm_split(a, b16):
    high, low = split(a)
    return mm(high, b16) + mm(low, b16)


def lanes_sum(value, tri):
    first = value.astype(BF16)
    rest = value - first.astype(F32)
    second = rest.astype(BF16)
    third = (rest - second.astype(F32)).astype(BF16)
    return mm(first, tri) + mm(second, tri) + mm(third, tri)


def kernel(
    x_hbm, g_hbm, b_hbm, c_hbm, dec_hbm, lw_hbm, fsg_hbm,
    up_out, db_out, dc_out, wg_out, dg_out,
    xa, ga, ba, ca, dec, lw, fsg,
    xt, gt, gt16, bt16, ct16,
    r_rows, e_rows, f_rows, a_rows, w_rows,
    ag, fx, sp, dp, attn, ups,
    dz, st, tot, dzi, sti, dso, zko, dto, dsf, zkf, dti,
    wg, dct, dbs, dcs, dbi, dci, wgs, dgs, xdx, near, low_dz, last, fin,
    a_send, a_recv, z_send, z_recv, n_send, n_recv, u_send, u_recv, o_send, o_recv, loc,
):
    seq = lax.axis_index("seq")
    sec = lax.axis_index("section")
    z = seq // NB
    q = lax.rem(seq, NB)
    before = lax.rem(sec + SECTIONS - 1, SECTIONS)
    after = lax.rem(sec + 1, SECTIONS)

    def at(zz, qq, section=sec):
        return {"seq": zz * NB + qq, "section": section}

    def remote(src, dst, send_sem, recv_sem, where):
        return pltpu.make_async_remote_copy(
            src_ref=src, dst_ref=dst, send_sem=send_sem, recv_sem=recv_sem,
            device_id=where, device_id_type=MESH,
        )

    barrier = pltpu.get_barrier_semaphore()

    def greet(where):
        pl.semaphore_signal(barrier, inc=1, device_id=where, device_id_type=MESH)

    for o in range(1, NB):
        greet(at(z, lax.rem(q + o, NB)))
    for o in range(1, NZ):
        greet(at(lax.rem(z + o, NZ), q))
    for i in range(NB):
        greet(at(z, i, before))
        greet(at(z, i, after))
    pl.semaphore_wait(barrier, NB - 1 + NZ - 1 + 2 * NB)

    def pair_at(j):
        return lax.rem(z // 2 + 1 + j, NB)

    def piece(kind, owner, slot, j):
        heads = pl.ds(pl.multiple_of(owner * HQ, HQ), HQ)
        there = pl.ds(pl.multiple_of(pair_at(j) * BLK, BLK), BLK)
        cols = pl.ds(pl.multiple_of(owner * COLS + pair_at(j) * BLK, BLK), BLK)
        rows = pl.ds(pl.multiple_of(slot * BLK, BLK), BLK)
        if kind == DEC:
            return dec_hbm.at[heads, :], dec.at[slot]
        if kind == LWT:
            return lw_hbm.at[:, heads, :], lw.at[slot]
        if kind == CPR:
            return c_hbm, ca.at[rows, :]
        if kind == GRD:
            return g_hbm.at[:, cols], ga.at[rows, there]
        if kind == BPR:
            return b_hbm, ba.at[rows, :]
        return x_hbm.at[:, cols], xa.at[rows, there]

    def group_send(kind, o, j):
        peer = lax.rem(q + o, NB)
        src, dst = piece(kind, peer, q, j)
        return remote(src, dst, a_send.at[kind, j, o], a_recv.at[kind, j, q], at(z, peer))

    def group_start(kind, j=0):
        for o in range(1, NB):
            group_send(kind, o, j).start()
        src, dst = piece(kind, q, q, j)
        pltpu.make_async_copy(src, dst, loc.at[kind, j]).start()

    def group_wait(kind, j=0):
        src, dst = piece(kind, q, q, j)
        pltpu.make_async_copy(src, dst, loc.at[kind, j]).wait()
        for o in range(1, NB):
            peer = lax.rem(q + o, NB)
            dst = piece(kind, peer, peer, j)[1]
            remote(dst, dst, a_send.at[kind, j, o], a_recv.at[kind, j, peer], at(z, peer)).wait_recv()

    for kind in (DEC, LWT, CPR):
        group_start(kind)
    for j in range(AHEAD):
        group_start(GRD, j)
    final_copy = pltpu.make_async_copy(fsg_hbm.at[pl.ds(pl.multiple_of(q * HQ, HQ), HQ)], fsg, loc.at[6, 0])
    final_copy.start()

    row_of = lax.broadcasted_iota(jnp.int32, (BLK, BLK), 0)
    col_of = lax.broadcasted_iota(jnp.int32, (BLK, BLK), 1)
    causal = row_of <= col_of
    upto = jnp.where(causal, 1.0, 0.0).astype(BF16)
    onward = jnp.where(row_of >= col_of, 1.0, 0.0).astype(BF16)
    left = lax.broadcasted_iota(jnp.int32, (BLK, BLK), 1) < HP

    group_wait(DEC)
    running = lanes_sum(jnp.concatenate([dec[i] for i in range(NB)], axis=0), upto)
    sofar = jnp.zeros((HQ, 1), F32)
    for i in range(NB):
        own = running[i * HQ : (i + 1) * HQ]
        r_rows[:, i * BLK : (i + 1) * BLK] = own + sofar
        sofar = sofar + own[:, BLK - 1 : BLK]
    tot[z] = jnp.broadcast_to(sofar, (HQ, BLK))

    def z_send_one(kind, peer, src, dst):
        return remote(src, dst, z_send.at[kind, peer], z_recv.at[kind, z], at(peer, q))

    def z_wait(kind, dst, peer):
        remote(dst, dst, z_send.at[kind, 0], z_recv.at[kind, peer], at(peer, q)).wait_recv()

    @pl.loop(1, NZ)
    def _(o):
        z_send_one(TOT, lax.rem(z + o, NZ), tot.at[z], tot.at[z]).start()

    r_all = r_rows[...]
    e_rows[...] = jnp.exp(r_all)
    f_rows[...] = jnp.exp(sofar - r_all)
    group_wait(LWT)
    for k in range(3):
        for i in range(NB):
            a_rows[k, :, i * BLK : (i + 1) * BLK] = lw[i, 3 + k] * e_rows[:, i * BLK : (i + 1) * BLK]
    for i in range(NB):
        for j in range(i, NB):
            w_rows[i, :, j * BLK : (j + 1) * BLK] = lw[j, level_of(i, j) + 1]

    group_wait(CPR)
    for i in range(NB):
        ct16[:, i * BLK : (i + 1) * BLK] = ca[i * BLK : (i + 1) * BLK, :].astype(F32).T.astype(BF16)
    wg[...] = jnp.zeros_like(wg)
    dp[...] = jnp.zeros_like(dp)

    def bit(zz, k):
        return lax.rem(zz // 2**k, 2) == 1

    def head_rows(h):
        return pl.ds(pl.multiple_of(h * HP, HP), HP)

    def pair_rows(p):
        return pl.ds(pl.multiple_of(p * BLK, BLK), BLK)

    def to_owners(kind, p, source, landing):
        for half in range(2):
            owner = 2 * p + half

            @pl.when(owner != z)
            def _(owner=owner):
                z_send_one(kind, owner, source.at[head_rows(owner), :], landing.at[z]).start()

            @pl.when(owner == z)
            def _(owner=owner):
                landing[z] = source[head_rows(owner), :]

    def down_send(p):
        return remote(dz.at[0, pair_rows(p), :], low_dz.at[pair_rows(p), :], n_send.at[0, p], n_recv.at[0, p], at(z - 1, q))

    def up_state(p):
        return remote(st.at[pair_rows(p), :], zkf.at[0, pair_rows(p), :], n_send.at[1, p], n_recv.at[1, p], at(z + 1, q))

    for k in range(3):

        @pl.when(jnp.logical_not(bit(z, k)))
        def _(k=k):
            zkf[k] = jnp.zeros((COLS, N), F32)

    @pl.when(z >= FED)
    def _():
        dsf[...] = jnp.zeros((COLS, N), F32)

    @pl.loop(0, NB)
    def _(j):
        p = pair_at(j)
        cols = pair_rows(p)
        group_wait(GRD, j)

        @pl.when(j < NB - AHEAD)
        def _():
            group_start(GRD, j + AHEAD)

        @pl.when(j == NB - AHEAD)
        def _():
            group_start(BPR)

        @pl.when(j >= NB - AHEAD)
        def _():
            group_start(INP, j + AHEAD - NB)

        for i in range(NB):
            rows = ga[i * BLK : (i + 1) * BLK, cols].astype(F32).T
            gt[cols, i * BLK : (i + 1) * BLK] = rows
            gt16[cols, i * BLK : (i + 1) * BLK] = rows.astype(BF16)
        for k in range(3):

            @pl.when(bit(z, k))
            def _(k=k):
                for half in range(2):
                    rows = head_rows(2 * p + half)
                    high, low = split(gt[rows, :] * a_rows[k, pl.ds(2 * p + half, 1), :])
                    ag[k, 0, rows, :] = high
                    ag[k, 1, rows, :] = low
                dz[k, cols, :] = mm(ag[k, 0, cols, :], ca[...]) + mm(ag[k, 1, cols, :], ca[...])
                if k == 0:
                    down_send(p).start()
                else:
                    to_owners(DZK + k, p, dz.at[k], dzi.at[k])

    group_wait(BPR)
    for i in range(NB):
        bt16[:, i * BLK : (i + 1) * BLK] = ba[i * BLK : (i + 1) * BLK, :].astype(F32).T.astype(BF16)

    @pl.loop(0, NB)
    def _(j):
        p = pair_at(j)
        cols = pair_rows(p)
        group_wait(INP, j)

        @pl.when(j < NB - AHEAD)
        def _():
            group_start(INP, j + AHEAD)

        for i in range(NB):
            xt[cols, i * BLK : (i + 1) * BLK] = xa[i * BLK : (i + 1) * BLK, cols].astype(F32).T
        for half in range(2):
            rows = head_rows(2 * p + half)
            high, low = split(xt[rows, :] * f_rows[pl.ds(2 * p + half, 1), :])
            fx[0, rows, :] = high
            fx[1, rows, :] = low
        st[cols, :] = mm(fx[0, cols, :], ba[...]) + mm(fx[1, cols, :], ba[...])

        @pl.when(jnp.logical_not(bit(z, 0)))
        def _():
            up_state(p).start()

        @pl.when(z < FED)
        def _():
            to_owners(STA, p, st, sti)

    sp[...] = mm(ba[...], ct16[...])

    @pl.loop(0, NB)
    def _(p):
        cols = pl.ds(pl.multiple_of(p * BLK, BLK), BLK)
        runs = [r_rows[pl.ds(2 * p + half, 1), :] for half in range(2)]
        found = [{(level, j): jnp.zeros((1, BLK), F32) for level in range(3) for j in range(NB)} for _ in range(2)]
        for i in range(NB):
            keys = slice(i * BLK, (i + 1) * BLK)
            pair = []
            for half in range(2):
                keep = left if half == 0 else jnp.logical_not(left)
                own = jnp.where(keep, xa[keys, cols].astype(F32), 0.0).astype(BF16)
                run = runs[half]
                weights = w_rows[i, pl.ds(2 * p + half, 1), :]
                r_keys = jnp.broadcast_to(run[:, keys], (BLK, BLK)).T
                grad = jnp.zeros((BLK, BLK), F32)
                for j in range(i, NB):
                    queries = slice(j * BLK, (j + 1) * BLK)
                    product = mm(own, gt16[cols, queries])
                    spread = run[:, queries] - r_keys
                    if i == j:
                        spread = jnp.where(causal, spread, -1e30)
                    decay = jnp.exp(spread)
                    score = sp[keys, queries]
                    level = level_of(i, j) + 1
                    found[half][level, j] += jnp.sum(product * decay * score, axis=0, keepdims=True)
                    decay = decay * weights[:, queries]
                    dp[keys, queries] += product * decay
                    grad = grad + mm_split(score * decay, ga[queries, cols])
                pair.append(grad)
            attn[cols, keys] = jnp.where(left, pair[0], pair[1]).T
        for half in range(2):
            for level in range(3):
                row = jnp.concatenate([found[half][level, j] for j in range(NB)], axis=1)
                wg[level, pl.ds(2 * p + half, 1), :] = row

    high, low = split(dp[...])
    dct[...] = mm(bt16[...], high) + mm(bt16[...], low)
    for i in range(NB):
        dbs[i] = mm_split(dp[i * BLK : (i + 1) * BLK, :], ca[...])

    @pl.loop(1, NZ)
    def _(o):
        peer = lax.rem(z + o, NZ)
        z_wait(TOT, tot.at[peer], peer)

    for k in range(1, 3):

        @pl.loop(1, NZ)
        def _(o, k=k):
            peer = lax.rem(z + o, NZ)

            @pl.when(bit(peer, k))
            def _():
                z_wait(DZK + k, dzi.at[k, peer], peer)

    totals = [tot[d, pl.ds(z, 1), :] for d in range(NZ)]
    weight = {}
    for e in range(FED):
        gap = jnp.zeros((1, BLK), F32)
        for d in range(e + 1, NZ):
            weight[e, d] = jnp.exp(gap)
            gap = gap + totals[d]
    for e in range(FED):
        grad = jnp.zeros((HP, N), F32)
        for d in range(e + 1, NZ):
            if level_of(e, d) > 0:
                grad = grad + weight[e, d] * dzi[level_of(e, d), d]
        dso[e] = grad

    @pl.when(z < FED)
    def _():
        dsf[head_rows(z), :] = dso[z]

    @pl.loop(1, NZ)
    def _(o):
        peer = lax.rem(z + o, NZ)

        @pl.when(peer < FED)
        def _():
            z_send_one(DST, peer, dso.at[peer], dsf.at[head_rows(z), :]).start()

    @pl.loop(1, NZ)
    def _(o):
        peer = lax.rem(z + o, NZ)

        @pl.when(peer < FED)
        def _():
            z_wait(STA, sti.at[peer], peer)

    for d in range(1, NZ):
        for k in range(1, 3):
            if d >> k & 1:
                base = d - d % 2 ** (k + 1)
                carry = jnp.zeros((HP, N), F32)
                for e in range(base, base + 2**k):
                    carry = carry + weight[e, d] * sti[e]
                zko[k, d] = carry

    for k in range(1, 3):

        @pl.when(bit(z, k))
        def _(k=k):
            zkf[k, head_rows(z), :] = zko[k, z]

        @pl.loop(1, NZ)
        def _(o, k=k):
            peer = lax.rem(z + o, NZ)

            @pl.when(bit(peer, k))
            def _():
                z_send_one(ZKK + k, peer, zko.at[k, peer], zkf.at[k, head_rows(z), :]).start()

    def fold(value):
        return sum(value[8 * i : 8 * (i + 1)] for i in range(HP // 8))

    across = [jnp.zeros((8, N), F32) for _ in range(NZ)]
    for e in range(FED):
        for d in range(e + 1, NZ):
            if level_of(e, d) == 0:
                continue
            shared = weight[e, d] * fold(sti[e] * dzi[level_of(e, d), d])
            for f in range(e, d):
                across[f] = across[f] + shared
    for f in range(NZ):
        dto[f] = across[f]
    dti[z] = dto[z]

    @pl.loop(1, NZ)
    def _(o):
        peer = lax.rem(z + o, NZ)
        z_send_one(DTT, peer, dto.at[peer], dti.at[z]).start()

    def carried_level(k):
        @pl.when(bit(z, k))
        def _():
            if k == 0:
                for p in range(NB):
                    there = zkf.at[0, pair_rows(p), :]
                    remote(there, there, n_send.at[1, p], n_recv.at[1, p], at(z - 1, q)).wait_recv()
            else:

                @pl.loop(1, NZ)
                def _(o):
                    peer = lax.rem(z + o, NZ)
                    z_wait(ZKK + k, zkf.at[k, head_rows(peer), :], peer)

            @pl.loop(0, NB)
            def _(p):
                cols = pl.ds(pl.multiple_of(p * BLK, BLK), BLK)
                reach = mm_split(zkf[k, cols, :], ct16[...]) * gt[cols, :]
                for half in range(2):
                    h = 2 * p + half
                    row = jnp.sum(reach[half * HP : (half + 1) * HP], axis=0, keepdims=True)
                    wg[3 + k, pl.ds(h, 1), :] = row * e_rows[pl.ds(h, 1), :]

            high, low = split(jnp.concatenate([zkf[k, c * BLK : (c + 1) * BLK, :].T for c in range(NB)], axis=1))
            dct[...] += mm(high, ag[k, 0]) + mm(low, ag[k, 0]) + mm(high, ag[k, 1])

    for p in range(NB):

        @pl.when(jnp.logical_not(bit(z, 0)))
        def _(p=p):
            there = low_dz.at[pair_rows(p), :]
            remote(there, there, n_send.at[0, p], n_recv.at[0, p], at(z + 1, q)).wait_recv()

        @pl.when(bit(z, 0))
        def _(p=p):
            low_dz[p * BLK : (p + 1) * BLK, :] = jnp.zeros((BLK, N), F32)

    def per_pair(rows):
        return jnp.concatenate([jnp.broadcast_to(row, (HP, N)) for row in rows], axis=0)

    final_copy.wait()
    rest = jnp.zeros((HQ, N), F32)
    for f in range(1, NZ):
        rest = rest + tot[f] * jnp.where(z < f, 1.0, 0.0)
    fin[...] = jnp.exp(rest)

    def upstream_send(p, i):
        there = up_out.at[:, pl.ds(pl.multiple_of(q * COLS + p * BLK, BLK), BLK)]
        here = ups.at[i * BLK : (i + 1) * BLK, pair_rows(p)]
        return remote(here, there, u_send.at[p, i], u_recv.at[p, q], at(z, i, before))

    @pl.loop(0, NB)
    def _(j):
        p = pair_at(j)
        cols = pair_rows(p)
        for half in range(2):
            owner = 2 * p + half

            @pl.when(jnp.logical_and(z < FED, owner != z))
            def _(owner=owner):
                z_wait(DST, dsf.at[head_rows(owner), :], owner)

        ending = per_pair([fin[pl.ds(2 * p + half, 1), :] for half in range(2)])
        ending = ending * fsg[pl.ds(2 * p, 2)].reshape(BLK, N)
        last[cols, :] = ending
        state = dsf[cols, :] + low_dz[cols, :] + ending
        dsf[cols, :] = state
        spread = mm_split(state, bt16[...])
        factor = jnp.concatenate(
            [jnp.broadcast_to(f_rows[pl.ds(2 * p + half, 1), :], (HP, TOK)) for half in range(2)], axis=0
        )
        grad = attn[cols, :] + factor * spread
        own = grad * xt[cols, :]
        for half in range(2):
            part = slice(half * HP, (half + 1) * HP)
            xdx[pl.ds(2 * p + half, 1), :] = jnp.sum(own[part], axis=0, keepdims=True)
        for i in range(NB):
            ups[i * BLK : (i + 1) * BLK, cols] = grad[:, i * BLK : (i + 1) * BLK].T.astype(BF16)
        for i in range(NB):
            upstream_send(p, i).start()

    carried_level(0)

    db_t = jnp.zeros((N, TOK), F32)
    high, low = split(jnp.concatenate([dsf[c * BLK : (c + 1) * BLK, :].T for c in range(NB)], axis=1))
    db_t = mm(high, fx[0]) + mm(low, fx[0]) + mm(high, fx[1])
    for i in range(NB):
        keys = slice(i * BLK, (i + 1) * BLK)
        dbs[i] += db_t[:, keys].T

    def sum_send(kind, o):
        peer = lax.rem(q + o, NB)
        src, dst = ((dbs, dbi), (dcs, dci))[kind]
        return remote(src.at[peer], dst.at[q], o_send.at[kind, o], o_recv.at[kind, q], at(z, peer))

    for o in range(1, NB):
        sum_send(0, o).start()
    dbi[q] = dbs[q]

    for k in (1, 2):
        carried_level(k)

    dc_t = dct[...]
    for i in range(NB):
        dcs[i] = dc_t[:, i * BLK : (i + 1) * BLK].T
    for o in range(1, NB):
        sum_send(1, o).start()
    dci[q] = dcs[q]

    @pl.loop(1, NZ)
    def _(o):
        peer = lax.rem(z + o, NZ)
        z_wait(DTT, dti.at[peer], peer)

    @pl.loop(0, NB)
    def _(p):
        rows = pair_rows(p)
        decay = per_pair([jnp.exp(tot[z, pl.ds(2 * p + half, 1), :]) for half in range(2)])
        ended = decay * (zkf[0, rows, :] + zkf[1, rows, :] + zkf[2, rows, :]) + st[rows, :]
        own = st[rows, :] * low_dz[rows, :] + ended * last[rows, :]
        for half in range(2):
            part = slice(half * HP, (half + 1) * HP)
            near[pl.ds(2 * p + half, 1), :] = jnp.sum(own[part], axis=0, keepdims=True)

    crossing = jnp.concatenate([jnp.sum(dti[h], axis=0, keepdims=True) for h in range(HQ)], axis=0)
    later = jnp.sum(crossing + near[...], axis=1, keepdims=True)
    pieces = []
    for i in range(NB):
        here = slice(i * BLK, (i + 1) * BLK)
        change = -xdx[:, here]
        for level in range(6):
            change = change + lw[i, level] * wg[level, :, here]
            wgs[i, level] = wg[level, :, here]
        pieces.append(change)
    sums = lanes_sum(jnp.concatenate(pieces, axis=0), onward)
    for i in reversed(range(NB)):
        own = sums[i * HQ : (i + 1) * HQ]
        dgs[i] = own + later
        later = later + own[:, :1]

    mine = pl.ds(pl.multiple_of(q * HQ, HQ), HQ)

    def rows_send(kind, o):
        peer = lax.rem(q + o, NB)
        src, dst = (wgs.at[peer], wg_out.at[:, mine, :]) if kind == 2 else (dgs.at[peer], dg_out.at[mine, :])
        return remote(src, dst, o_send.at[kind, o], o_recv.at[kind, q], at(z, peer))

    for o in range(1, NB):
        rows_send(2, o).start()
        rows_send(3, o).start()
    own_wg = pltpu.make_async_copy(wgs.at[q], wg_out.at[:, mine, :], loc.at[6, 1])
    own_dg = pltpu.make_async_copy(dgs.at[q], dg_out.at[mine, :], loc.at[6, 2])
    own_wg.start()
    own_dg.start()

    for kind, landed in ((0, dbi), (1, dci)):
        for o in range(1, NB):
            peer = lax.rem(q + o, NB)
            there = landed.at[peer]
            remote(there, there, o_send.at[kind, o], o_recv.at[kind, peer], at(z, peer)).wait_recv()
    db_out[...] = dbi[0] + dbi[1] + dbi[2] + dbi[3]
    dc_out[...] = dci[0] + dci[1] + dci[2] + dci[3]

    own_wg.wait()
    own_dg.wait()
    for o in range(1, NB):
        peer = lax.rem(q + o, NB)
        theirs = pl.ds(pl.multiple_of(peer * HQ, HQ), HQ)
        for kind, there in ((2, wg_out.at[:, theirs, :]), (3, dg_out.at[theirs, :])):
            remote(there, there, o_send.at[kind, o], o_recv.at[kind, peer], at(z, peer)).wait_recv()
    for i in range(NB):
        for p in range(NB):
            there = up_out.at[:, i * COLS + p * BLK : i * COLS + (p + 1) * BLK]
            remote(there, there, u_send.at[p, i], u_recv.at[p, i], at(z, i, after)).wait_recv()

    for o in range(1, NB):
        for kind in (DEC, LWT, CPR, BPR):
            group_send(kind, o, 0).wait_send()
        for j in range(NB):
            group_send(GRD, o, j).wait_send()
            group_send(INP, o, j).wait_send()
        sum_send(0, o).wait_send()
        sum_send(1, o).wait_send()
        rows_send(2, o).wait_send()
        rows_send(3, o).wait_send()
    for p in range(NB):
        for i in range(NB):
            upstream_send(p, i).wait_send()

        @pl.when(bit(z, 0))
        def _(p=p):
            down_send(p).wait_send()

        @pl.when(jnp.logical_not(bit(z, 0)))
        def _(p=p):
            up_state(p).wait_send()

    @pl.loop(1, NZ)
    def _(o):
        peer = lax.rem(z + o, NZ)
        z_send_one(TOT, peer, tot.at[z], tot.at[z]).wait_send()

        @pl.when(z < FED)
        def _():
            z_send_one(STA, peer, st.at[head_rows(peer), :], sti.at[z]).wait_send()

        @pl.when(peer < FED)
        def _():
            z_send_one(DST, peer, dso.at[peer], dsf.at[head_rows(z), :]).wait_send()

        z_send_one(DTT, peer, dto.at[peer], dti.at[z]).wait_send()
        for k in range(1, 3):

            @pl.when(bit(z, k))
            def _(k=k):
                z_send_one(DZK + k, peer, dz.at[k, head_rows(peer), :], dzi.at[k, z]).wait_send()

            @pl.when(bit(peer, k))
            def _(k=k):
                z_send_one(ZKK + k, peer, zko.at[k, peer], zkf.at[k, head_rows(z), :]).wait_send()


def hand_over(*refs):
    sources, targets, held, sem = refs[:5], refs[5:10], refs[10:15], refs[15]
    taken = [pltpu.make_async_copy(src, mid, sem.at[0, i]) for i, (src, mid) in enumerate(zip(sources, held))]
    given = [pltpu.make_async_copy(mid, dst, sem.at[1, i]) for i, (mid, dst) in enumerate(zip(held, targets))]
    for copy in taken:
        copy.start()
    for first, second in zip(taken, given):
        first.wait()
        second.start()
    for copy in given:
        copy.wait()


def body(inputs, b_proj, c_proj, decay_log, level_weight, out_grad, final_state_grad):
    def vmem(*shape, dtype=F32):
        return pltpu.VMEM(shape, dtype)

    scratch = [
        vmem(TOK, COLS, dtype=BF16),
        vmem(TOK, COLS, dtype=BF16),
        vmem(TOK, N, dtype=BF16),
        vmem(TOK, N, dtype=BF16),
        vmem(NB, HQ, BLK),
        vmem(NB, 6, HQ, BLK),
        vmem(HQ, HP, N),
        vmem(COLS, TOK),
        vmem(COLS, TOK),
        vmem(COLS, TOK, dtype=BF16),
        vmem(N, TOK, dtype=BF16),
        vmem(N, TOK, dtype=BF16),
        vmem(HQ, TOK),
        vmem(HQ, TOK),
        vmem(HQ, TOK),
        vmem(3, HQ, TOK),
        vmem(NB, HQ, TOK),
        vmem(3, 2, COLS, TOK, dtype=BF16),
        vmem(2, COLS, TOK, dtype=BF16),
        vmem(TOK, TOK),
        vmem(TOK, TOK),
        vmem(COLS, TOK),
        vmem(TOK, COLS, dtype=BF16),
        vmem(3, COLS, N),
        vmem(COLS, N),
        vmem(NZ, HQ, BLK),
        vmem(3, NZ, HP, N),
        vmem(NZ, HP, N),
        vmem(NZ, HP, N),
        vmem(3, NZ, HP, N),
        vmem(NZ, 8, N),
        vmem(COLS, N),
        vmem(3, COLS, N),
        vmem(NZ, 8, N),
        vmem(6, HQ, TOK),
        vmem(N, TOK),
        vmem(NB, BLK, N),
        vmem(NB, BLK, N),
        vmem(NB, BLK, N),
        vmem(NB, BLK, N),
        vmem(NB, 6, HQ, BLK),
        vmem(NB, HQ, BLK),
        vmem(HQ, TOK),
        vmem(HQ, N),
        vmem(COLS, N),
        vmem(COLS, N),
        vmem(HQ, N),
        pltpu.SemaphoreType.DMA((6, NB, NB)),
        pltpu.SemaphoreType.DMA((6, NB, NB)),
        pltpu.SemaphoreType.DMA((10, NZ)),
        pltpu.SemaphoreType.DMA((10, NZ)),
        pltpu.SemaphoreType.DMA((2, NB)),
        pltpu.SemaphoreType.DMA((2, NB)),
        pltpu.SemaphoreType.DMA((NB, NB)),
        pltpu.SemaphoreType.DMA((NB, NB)),
        pltpu.SemaphoreType.DMA((4, NB)),
        pltpu.SemaphoreType.DMA((4, NB)),
        pltpu.SemaphoreType.DMA((7, NB)),
    ]
    anywhere = pl.BlockSpec(memory_space=pl.ANY)
    made = (
        jax.ShapeDtypeStruct((BLK, HEADS * HP), BF16),
        jax.ShapeDtypeStruct((BLK, N), F32),
        jax.ShapeDtypeStruct((BLK, N), F32),
        jax.ShapeDtypeStruct((6, HEADS, BLK), F32),
        jax.ShapeDtypeStruct((HEADS, BLK), F32),
    )
    results = pl.pallas_call(
        kernel,
        out_shape=made,
        in_specs=[anywhere] * 7,
        out_specs=(anywhere, pl.BlockSpec(memory_space=pltpu.VMEM), pl.BlockSpec(memory_space=pltpu.VMEM), anywhere, anywhere),
        scratch_shapes=scratch,
        compiler_params=pltpu.CompilerParams(
            collective_id=0, has_side_effects=True, vmem_limit_bytes=56 * 2**20
        ),
    )(
        inputs[0],
        out_grad[0],
        b_proj[0],
        c_proj[0],
        decay_log[0].T,
        jnp.transpose(level_weight[0], (1, 2, 0)),
        jnp.transpose(final_state_grad[0], (0, 2, 1)),
    )
    up, db, dc, wg, dg = pl.pallas_call(
        hand_over,
        out_shape=made,
        in_specs=[anywhere] * 5,
        out_specs=[anywhere] * 5,
        scratch_shapes=[*(pltpu.VMEM(m.shape, m.dtype) for m in made), pltpu.SemaphoreType.DMA((2, 5))],
        compiler_params=pltpu.CompilerParams(vmem_limit_bytes=56 * 2**20),
    )(*results)
    return (up[None], db[None], dc[None], dg.T[None], jnp.transpose(wg, (2, 0, 1))[None])


def solution(mesh):
    rows = P("section", "seq", None)
    deep = P("section", "seq", None, None)
    return jax.shard_map(
        body,
        mesh=mesh,
        in_specs=(rows, rows, rows, rows, deep, rows, P("section", None, None, None)),
        out_specs=(rows, rows, rows, rows, deep),
        check_vma=False,
    )
```

```python
import jax
import jax.numpy as jnp
from jax import lax
from jax.experimental import pallas as pl
from jax.experimental.pallas import tpu as pltpu
from jax.sharding import PartitionSpec as P

MESH = pl.DeviceIdType.MESH
F32, BF16 = jnp.float32, jnp.bfloat16
BLK = 128
NB = 4
NZ = 8
HEADS = 32
HQ = HEADS // NB
HP = 64
N = 128
TOK = NB * BLK
COLS = HQ * HP
SECTIONS = 8
AHEAD = 4
FED = 6
DEC, LWT, CPR, GRD, BPR, INP = range(6)
TOT, DZK, STA, DST, ZKK, DTT = 0, 1, 4, 5, 6, 9


def level_of(low, high):
    return (low ^ high).bit_length() - 1


def split(value):
    high = value.astype(BF16)
    return high, (value - high.astype(F32)).astype(BF16)


def mm(a, b):
    return jnp.dot(a, b, preferred_element_type=F32)


def mm_split(a, b16):
    high, low = split(a)
    return mm(high, b16) + mm(low, b16)


def lanes_sum(value, tri):
    first = value.astype(BF16)
    rest = value - first.astype(F32)
    second = rest.astype(BF16)
    third = (rest - second.astype(F32)).astype(BF16)
    return mm(first, tri) + mm(second, tri) + mm(third, tri)


def kernel(
    x_hbm, g_hbm, b_hbm, c_hbm, dec_hbm, lw_hbm, fsg_hbm,
    up_out, db_out, dc_out, wg_out, dg_out,
    xa, ga, ba, ca, dec, lw, fsg,
    xt, gt, gt16, bt16, ct16,
    r_rows, e_rows, f_rows, a_rows, w_rows,
    ag, fx, sp, dp, attn, ups,
    dz, st, tot, dzi, sti, dso, zko, dto, dsf, zkf, dti,
    wg, dct, dbs, dcs, dbi, dci, wgs, dgs, xdx, near, low_dz, last, fin, summed,
    a_send, a_recv, z_send, z_recv, n_send, n_recv, u_send, u_recv, o_send, o_recv, loc,
):
    seq = lax.axis_index("seq")
    sec = lax.axis_index("section")
    z = seq // NB
    q = lax.rem(seq, NB)
    before = lax.rem(sec + SECTIONS - 1, SECTIONS)
    after = lax.rem(sec + 1, SECTIONS)

    def at(zz, qq, section=sec):
        return {"seq": zz * NB + qq, "section": section}

    def remote(src, dst, send_sem, recv_sem, where):
        return pltpu.make_async_remote_copy(
            src_ref=src, dst_ref=dst, send_sem=send_sem, recv_sem=recv_sem,
            device_id=where, device_id_type=MESH,
        )

    barrier = pltpu.get_barrier_semaphore()

    def greet(where):
        pl.semaphore_signal(barrier, inc=1, device_id=where, device_id_type=MESH)

    for o in range(1, NB):
        greet(at(z, lax.rem(q + o, NB)))
    for o in range(1, NZ):
        greet(at(lax.rem(z + o, NZ), q))
    for i in range(NB):
        greet(at(z, i, before))
        greet(at(z, i, after))
    pl.semaphore_wait(barrier, NB - 1 + NZ - 1 + 2 * NB)

    def pair_at(j):
        return lax.rem(z // 2 + 1 + j, NB)

    def piece(kind, owner, slot, j):
        heads = pl.ds(pl.multiple_of(owner * HQ, HQ), HQ)
        there = pl.ds(pl.multiple_of(pair_at(j) * BLK, BLK), BLK)
        cols = pl.ds(pl.multiple_of(owner * COLS + pair_at(j) * BLK, BLK), BLK)
        rows = pl.ds(pl.multiple_of(slot * BLK, BLK), BLK)
        if kind == DEC:
            return dec_hbm.at[heads, :], dec.at[slot]
        if kind == LWT:
            return lw_hbm.at[:, heads, :], lw.at[slot]
        if kind == CPR:
            return c_hbm, ca.at[rows, :]
        if kind == GRD:
            return g_hbm.at[:, cols], ga.at[rows, there]
        if kind == BPR:
            return b_hbm, ba.at[rows, :]
        return x_hbm.at[:, cols], xa.at[rows, there]

    def group_send(kind, o, j):
        peer = lax.rem(q + o, NB)
        src, dst = piece(kind, peer, q, j)
        return remote(src, dst, a_send.at[kind, j, o], a_recv.at[kind, j, q], at(z, peer))

    def group_start(kind, j=0):
        for o in range(1, NB):
            group_send(kind, o, j).start()
        src, dst = piece(kind, q, q, j)
        pltpu.make_async_copy(src, dst, loc.at[kind, j]).start()

    def group_wait(kind, j=0):
        src, dst = piece(kind, q, q, j)
        pltpu.make_async_copy(src, dst, loc.at[kind, j]).wait()
        for o in range(1, NB):
            peer = lax.rem(q + o, NB)
            dst = piece(kind, peer, peer, j)[1]
            remote(dst, dst, a_send.at[kind, j, o], a_recv.at[kind, j, peer], at(z, peer)).wait_recv()

    for kind in (DEC, LWT, CPR):
        group_start(kind)
    for j in range(AHEAD):
        group_start(GRD, j)
    final_copy = pltpu.make_async_copy(fsg_hbm.at[pl.ds(pl.multiple_of(q * HQ, HQ), HQ)], fsg, loc.at[6, 0])
    final_copy.start()

    row_of = lax.broadcasted_iota(jnp.int32, (BLK, BLK), 0)
    col_of = lax.broadcasted_iota(jnp.int32, (BLK, BLK), 1)
    causal = row_of <= col_of
    upto = jnp.where(causal, 1.0, 0.0).astype(BF16)
    onward = jnp.where(row_of >= col_of, 1.0, 0.0).astype(BF16)
    left = lax.broadcasted_iota(jnp.int32, (BLK, BLK), 1) < HP

    group_wait(DEC)
    running = lanes_sum(jnp.concatenate([dec[i] for i in range(NB)], axis=0), upto)
    sofar = jnp.zeros((HQ, 1), F32)
    for i in range(NB):
        own = running[i * HQ : (i + 1) * HQ]
        r_rows[:, i * BLK : (i + 1) * BLK] = own + sofar
        sofar = sofar + own[:, BLK - 1 : BLK]
    tot[z] = jnp.broadcast_to(sofar, (HQ, BLK))

    def z_send_one(kind, peer, src, dst):
        return remote(src, dst, z_send.at[kind, peer], z_recv.at[kind, z], at(peer, q))

    def z_wait(kind, dst, peer):
        remote(dst, dst, z_send.at[kind, 0], z_recv.at[kind, peer], at(peer, q)).wait_recv()

    @pl.loop(1, NZ)
    def _(o):
        z_send_one(TOT, lax.rem(z + o, NZ), tot.at[z], tot.at[z]).start()

    r_all = r_rows[...]
    e_rows[...] = jnp.exp(r_all)
    f_rows[...] = jnp.exp(sofar - r_all)
    group_wait(LWT)
    for k in range(3):
        for i in range(NB):
            a_rows[k, :, i * BLK : (i + 1) * BLK] = lw[i, 3 + k] * e_rows[:, i * BLK : (i + 1) * BLK]
    for i in range(NB):
        for j in range(i, NB):
            w_rows[i, :, j * BLK : (j + 1) * BLK] = lw[j, level_of(i, j) + 1]

    group_wait(CPR)
    for i in range(NB):
        ct16[:, i * BLK : (i + 1) * BLK] = ca[i * BLK : (i + 1) * BLK, :].astype(F32).T.astype(BF16)
    wg[...] = jnp.zeros_like(wg)
    dp[...] = jnp.zeros_like(dp)

    def bit(zz, k):
        return lax.rem(zz // 2**k, 2) == 1

    def head_rows(h):
        return pl.ds(pl.multiple_of(h * HP, HP), HP)

    def pair_rows(p):
        return pl.ds(pl.multiple_of(p * BLK, BLK), BLK)

    def to_owners(kind, p, source, landing):
        for half in range(2):
            owner = 2 * p + half

            @pl.when(owner != z)
            def _(owner=owner):
                z_send_one(kind, owner, source.at[head_rows(owner), :], landing.at[z]).start()

            @pl.when(owner == z)
            def _(owner=owner):
                landing[z] = source[head_rows(owner), :]

    def down_send(p):
        return remote(dz.at[0, pair_rows(p), :], low_dz.at[pair_rows(p), :], n_send.at[0, p], n_recv.at[0, p], at(z - 1, q))

    def up_state(p):
        return remote(st.at[pair_rows(p), :], zkf.at[0, pair_rows(p), :], n_send.at[1, p], n_recv.at[1, p], at(z + 1, q))

    for k in range(3):

        @pl.when(jnp.logical_not(bit(z, k)))
        def _(k=k):
            zkf[k] = jnp.zeros((COLS, N), F32)

    @pl.when(z >= FED)
    def _():
        dsf[...] = jnp.zeros((COLS, N), F32)

    @pl.loop(0, NB)
    def _(j):
        p = pair_at(j)
        cols = pair_rows(p)
        group_wait(GRD, j)

        @pl.when(j < NB - AHEAD)
        def _():
            group_start(GRD, j + AHEAD)

        @pl.when(j == NB - AHEAD)
        def _():
            group_start(BPR)

        @pl.when(j >= NB - AHEAD)
        def _():
            group_start(INP, j + AHEAD - NB)

        for i in range(NB):
            rows = ga[i * BLK : (i + 1) * BLK, cols].astype(F32).T
            gt[cols, i * BLK : (i + 1) * BLK] = rows
            gt16[cols, i * BLK : (i + 1) * BLK] = rows.astype(BF16)
        for k in range(3):

            @pl.when(bit(z, k))
            def _(k=k):
                for half in range(2):
                    rows = head_rows(2 * p + half)
                    high, low = split(gt[rows, :] * a_rows[k, pl.ds(2 * p + half, 1), :])
                    ag[k, 0, rows, :] = high
                    ag[k, 1, rows, :] = low
                dz[k, cols, :] = mm(ag[k, 0, cols, :], ca[...]) + mm(ag[k, 1, cols, :], ca[...])
                if k == 0:
                    down_send(p).start()
                else:
                    to_owners(DZK + k, p, dz.at[k], dzi.at[k])

    group_wait(BPR)
    for i in range(NB):
        bt16[:, i * BLK : (i + 1) * BLK] = ba[i * BLK : (i + 1) * BLK, :].astype(F32).T.astype(BF16)

    @pl.loop(0, NB)
    def _(j):
        p = pair_at(j)
        cols = pair_rows(p)
        group_wait(INP, j)

        @pl.when(j < NB - AHEAD)
        def _():
            group_start(INP, j + AHEAD)

        for i in range(NB):
            xt[cols, i * BLK : (i + 1) * BLK] = xa[i * BLK : (i + 1) * BLK, cols].astype(F32).T
        for half in range(2):
            rows = head_rows(2 * p + half)
            high, low = split(xt[rows, :] * f_rows[pl.ds(2 * p + half, 1), :])
            fx[0, rows, :] = high
            fx[1, rows, :] = low
        st[cols, :] = mm(fx[0, cols, :], ba[...]) + mm(fx[1, cols, :], ba[...])

        @pl.when(jnp.logical_not(bit(z, 0)))
        def _():
            up_state(p).start()

        @pl.when(z < FED)
        def _():
            to_owners(STA, p, st, sti)

    sp[...] = mm(ba[...], ct16[...])

    @pl.loop(0, NB)
    def _(p):
        cols = pl.ds(pl.multiple_of(p * BLK, BLK), BLK)
        runs = [r_rows[pl.ds(2 * p + half, 1), :] for half in range(2)]
        found = [{(level, j): jnp.zeros((1, BLK), F32) for level in range(3) for j in range(NB)} for _ in range(2)]
        for i in range(NB):
            keys = slice(i * BLK, (i + 1) * BLK)
            pair = []
            for half in range(2):
                keep = left if half == 0 else jnp.logical_not(left)
                own = jnp.where(keep, xa[keys, cols].astype(F32), 0.0).astype(BF16)
                run = runs[half]
                weights = w_rows[i, pl.ds(2 * p + half, 1), :]
                r_keys = jnp.broadcast_to(run[:, keys], (BLK, BLK)).T
                grad = jnp.zeros((BLK, BLK), F32)
                for j in range(i, NB):
                    queries = slice(j * BLK, (j + 1) * BLK)
                    product = mm(own, gt16[cols, queries])
                    spread = run[:, queries] - r_keys
                    if i == j:
                        spread = jnp.where(causal, spread, -1e30)
                    decay = jnp.exp(spread)
                    score = sp[keys, queries]
                    level = level_of(i, j) + 1
                    found[half][level, j] += jnp.sum(product * decay * score, axis=0, keepdims=True)
                    decay = decay * weights[:, queries]
                    dp[keys, queries] += product * decay
                    grad = grad + mm_split(score * decay, ga[queries, cols])
                pair.append(grad)
            attn[cols, keys] = jnp.where(left, pair[0], pair[1]).T
        for half in range(2):
            for level in range(3):
                row = jnp.concatenate([found[half][level, j] for j in range(NB)], axis=1)
                wg[level, pl.ds(2 * p + half, 1), :] = row

    high, low = split(dp[...])
    dct[...] = mm(bt16[...], high) + mm(bt16[...], low)
    for i in range(NB):
        dbs[i] = mm_split(dp[i * BLK : (i + 1) * BLK, :], ca[...])

    @pl.loop(1, NZ)
    def _(o):
        peer = lax.rem(z + o, NZ)
        z_wait(TOT, tot.at[peer], peer)

    for k in range(1, 3):

        @pl.loop(1, NZ)
        def _(o, k=k):
            peer = lax.rem(z + o, NZ)

            @pl.when(bit(peer, k))
            def _():
                z_wait(DZK + k, dzi.at[k, peer], peer)

    totals = [tot[d, pl.ds(z, 1), :] for d in range(NZ)]
    weight = {}
    for e in range(FED):
        gap = jnp.zeros((1, BLK), F32)
        for d in range(e + 1, NZ):
            weight[e, d] = jnp.exp(gap)
            gap = gap + totals[d]
    for e in range(FED):
        grad = jnp.zeros((HP, N), F32)
        for d in range(e + 1, NZ):
            if level_of(e, d) > 0:
                grad = grad + weight[e, d] * dzi[level_of(e, d), d]
        dso[e] = grad

    @pl.when(z < FED)
    def _():
        dsf[head_rows(z), :] = dso[z]

    @pl.loop(1, NZ)
    def _(o):
        peer = lax.rem(z + o, NZ)

        @pl.when(peer < FED)
        def _():
            z_send_one(DST, peer, dso.at[peer], dsf.at[head_rows(z), :]).start()

    @pl.loop(1, NZ)
    def _(o):
        peer = lax.rem(z + o, NZ)

        @pl.when(peer < FED)
        def _():
            z_wait(STA, sti.at[peer], peer)

    for d in range(1, NZ):
        for k in range(1, 3):
            if d >> k & 1:
                base = d - d % 2 ** (k + 1)
                carry = jnp.zeros((HP, N), F32)
                for e in range(base, base + 2**k):
                    carry = carry + weight[e, d] * sti[e]
                zko[k, d] = carry

    for k in range(1, 3):

        @pl.when(bit(z, k))
        def _(k=k):
            zkf[k, head_rows(z), :] = zko[k, z]

        @pl.loop(1, NZ)
        def _(o, k=k):
            peer = lax.rem(z + o, NZ)

            @pl.when(bit(peer, k))
            def _():
                z_send_one(ZKK + k, peer, zko.at[k, peer], zkf.at[k, head_rows(z), :]).start()

    def fold(value):
        return sum(value[8 * i : 8 * (i + 1)] for i in range(HP // 8))

    across = [jnp.zeros((8, N), F32) for _ in range(NZ)]
    for e in range(FED):
        for d in range(e + 1, NZ):
            if level_of(e, d) == 0:
                continue
            shared = weight[e, d] * fold(sti[e] * dzi[level_of(e, d), d])
            for f in range(e, d):
                across[f] = across[f] + shared
    for f in range(NZ):
        dto[f] = across[f]
    dti[z] = dto[z]

    @pl.loop(1, NZ)
    def _(o):
        peer = lax.rem(z + o, NZ)
        z_send_one(DTT, peer, dto.at[peer], dti.at[z]).start()

    def carried_level(k):
        @pl.when(bit(z, k))
        def _():
            if k == 0:
                for p in range(NB):
                    there = zkf.at[0, pair_rows(p), :]
                    remote(there, there, n_send.at[1, p], n_recv.at[1, p], at(z - 1, q)).wait_recv()
            else:

                @pl.loop(1, NZ)
                def _(o):
                    peer = lax.rem(z + o, NZ)
                    z_wait(ZKK + k, zkf.at[k, head_rows(peer), :], peer)

            @pl.loop(0, NB)
            def _(p):
                cols = pl.ds(pl.multiple_of(p * BLK, BLK), BLK)
                reach = mm_split(zkf[k, cols, :], ct16[...]) * gt[cols, :]
                for half in range(2):
                    h = 2 * p + half
                    row = jnp.sum(reach[half * HP : (half + 1) * HP], axis=0, keepdims=True)
                    wg[3 + k, pl.ds(h, 1), :] = row * e_rows[pl.ds(h, 1), :]

            high, low = split(jnp.concatenate([zkf[k, c * BLK : (c + 1) * BLK, :].T for c in range(NB)], axis=1))
            dct[...] += mm(high, ag[k, 0]) + mm(low, ag[k, 0]) + mm(high, ag[k, 1])

    for p in range(NB):

        @pl.when(jnp.logical_not(bit(z, 0)))
        def _(p=p):
            there = low_dz.at[pair_rows(p), :]
            remote(there, there, n_send.at[0, p], n_recv.at[0, p], at(z + 1, q)).wait_recv()

        @pl.when(bit(z, 0))
        def _(p=p):
            low_dz[p * BLK : (p + 1) * BLK, :] = jnp.zeros((BLK, N), F32)

    def per_pair(rows):
        return jnp.concatenate([jnp.broadcast_to(row, (HP, N)) for row in rows], axis=0)

    final_copy.wait()
    rest = jnp.zeros((HQ, N), F32)
    for f in range(1, NZ):
        rest = rest + tot[f] * jnp.where(z < f, 1.0, 0.0)
    fin[...] = jnp.exp(rest)

    def upstream_send(p, i):
        there = up_out.at[:, pl.ds(pl.multiple_of(q * COLS + p * BLK, BLK), BLK)]
        here = ups.at[i * BLK : (i + 1) * BLK, pair_rows(p)]
        return remote(here, there, u_send.at[p, i], u_recv.at[p, q], at(z, i, before))

    @pl.loop(0, NB)
    def _(j):
        p = pair_at(j)
        cols = pair_rows(p)
        for half in range(2):
            owner = 2 * p + half

            @pl.when(jnp.logical_and(z < FED, owner != z))
            def _(owner=owner):
                z_wait(DST, dsf.at[head_rows(owner), :], owner)

        ending = per_pair([fin[pl.ds(2 * p + half, 1), :] for half in range(2)])
        ending = ending * fsg[pl.ds(2 * p, 2)].reshape(BLK, N)
        last[cols, :] = ending
        state = dsf[cols, :] + low_dz[cols, :] + ending
        dsf[cols, :] = state
        spread = mm_split(state, bt16[...])
        factor = jnp.concatenate(
            [jnp.broadcast_to(f_rows[pl.ds(2 * p + half, 1), :], (HP, TOK)) for half in range(2)], axis=0
        )
        grad = attn[cols, :] + factor * spread
        own = grad * xt[cols, :]
        for half in range(2):
            part = slice(half * HP, (half + 1) * HP)
            xdx[pl.ds(2 * p + half, 1), :] = jnp.sum(own[part], axis=0, keepdims=True)
        for i in range(NB):
            ups[i * BLK : (i + 1) * BLK, cols] = grad[:, i * BLK : (i + 1) * BLK].T.astype(BF16)
        for i in range(NB):
            upstream_send(p, i).start()

    carried_level(0)

    db_t = jnp.zeros((N, TOK), F32)
    high, low = split(jnp.concatenate([dsf[c * BLK : (c + 1) * BLK, :].T for c in range(NB)], axis=1))
    db_t = mm(high, fx[0]) + mm(low, fx[0]) + mm(high, fx[1])
    for i in range(NB):
        keys = slice(i * BLK, (i + 1) * BLK)
        dbs[i] += db_t[:, keys].T

    def sum_send(kind, o):
        peer = lax.rem(q + o, NB)
        src, dst = ((dbs, dbi), (dcs, dci))[kind]
        return remote(src.at[peer], dst.at[q], o_send.at[kind, o], o_recv.at[kind, q], at(z, peer))

    for o in range(1, NB):
        sum_send(0, o).start()
    dbi[q] = dbs[q]

    for k in (1, 2):
        carried_level(k)

    dc_t = dct[...]
    for i in range(NB):
        dcs[i] = dc_t[:, i * BLK : (i + 1) * BLK].T
    for o in range(1, NB):
        sum_send(1, o).start()
    dci[q] = dcs[q]

    @pl.loop(1, NZ)
    def _(o):
        peer = lax.rem(z + o, NZ)
        z_wait(DTT, dti.at[peer], peer)

    @pl.loop(0, NB)
    def _(p):
        rows = pair_rows(p)
        decay = per_pair([jnp.exp(tot[z, pl.ds(2 * p + half, 1), :]) for half in range(2)])
        ended = decay * (zkf[0, rows, :] + zkf[1, rows, :] + zkf[2, rows, :]) + st[rows, :]
        own = st[rows, :] * low_dz[rows, :] + ended * last[rows, :]
        for half in range(2):
            part = slice(half * HP, (half + 1) * HP)
            near[pl.ds(2 * p + half, 1), :] = jnp.sum(own[part], axis=0, keepdims=True)

    crossing = jnp.concatenate([jnp.sum(dti[h], axis=0, keepdims=True) for h in range(HQ)], axis=0)
    later = jnp.sum(crossing + near[...], axis=1, keepdims=True)
    pieces = []
    for i in range(NB):
        here = slice(i * BLK, (i + 1) * BLK)
        change = -xdx[:, here]
        for level in range(6):
            change = change + lw[i, level] * wg[level, :, here]
            wgs[i, level] = wg[level, :, here]
        pieces.append(change)
    sums = lanes_sum(jnp.concatenate(pieces, axis=0), onward)
    for i in reversed(range(NB)):
        own = sums[i * HQ : (i + 1) * HQ]
        dgs[i] = own + later
        later = later + own[:, :1]

    mine = pl.ds(pl.multiple_of(q * HQ, HQ), HQ)

    def rows_send(kind, o):
        peer = lax.rem(q + o, NB)
        src, dst = (wgs.at[peer], wg_out.at[:, mine, :]) if kind == 2 else (dgs.at[peer], dg_out.at[mine, :])
        return remote(src, dst, o_send.at[kind, o], o_recv.at[kind, q], at(z, peer))

    for o in range(1, NB):
        rows_send(2, o).start()
        rows_send(3, o).start()
    own_wg = pltpu.make_async_copy(wgs.at[q], wg_out.at[:, mine, :], loc.at[6, 1])
    own_dg = pltpu.make_async_copy(dgs.at[q], dg_out.at[mine, :], loc.at[6, 2])
    own_wg.start()
    own_dg.start()

    for kind, landed in ((0, dbi), (1, dci)):
        for o in range(1, NB):
            peer = lax.rem(q + o, NB)
            there = landed.at[peer]
            remote(there, there, o_send.at[kind, o], o_recv.at[kind, peer], at(z, peer)).wait_recv()
        summed[kind] = landed[0] + landed[1] + landed[2] + landed[3]
        pltpu.make_async_copy(summed.at[kind], (db_out, dc_out)[kind], loc.at[7, kind]).start()

    own_wg.wait()
    own_dg.wait()
    late_db = pltpu.make_async_copy(summed.at[0], db_out, loc.at[7, 0])
    late_dc = pltpu.make_async_copy(summed.at[1], dc_out, loc.at[7, 1])
    for o in range(1, NB):
        peer = lax.rem(q + o, NB)
        theirs = pl.ds(pl.multiple_of(peer * HQ, HQ), HQ)
        for kind, there in ((2, wg_out.at[:, theirs, :]), (3, dg_out.at[theirs, :])):
            remote(there, there, o_send.at[kind, o], o_recv.at[kind, peer], at(z, peer)).wait_recv()
    for i in range(NB):
        for p in range(NB):
            there = up_out.at[:, i * COLS + p * BLK : i * COLS + (p + 1) * BLK]
            remote(there, there, u_send.at[p, i], u_recv.at[p, i], at(z, i, after)).wait_recv()

    late_db.wait()
    late_dc.wait()

    for o in range(1, NB):
        for kind in (DEC, LWT, CPR, BPR):
            group_send(kind, o, 0).wait_send()
        for j in range(NB):
            group_send(GRD, o, j).wait_send()
            group_send(INP, o, j).wait_send()
        sum_send(0, o).wait_send()
        sum_send(1, o).wait_send()
        rows_send(2, o).wait_send()
        rows_send(3, o).wait_send()
    for p in range(NB):
        for i in range(NB):
            upstream_send(p, i).wait_send()

        @pl.when(bit(z, 0))
        def _(p=p):
            down_send(p).wait_send()

        @pl.when(jnp.logical_not(bit(z, 0)))
        def _(p=p):
            up_state(p).wait_send()

    @pl.loop(1, NZ)
    def _(o):
        peer = lax.rem(z + o, NZ)
        z_send_one(TOT, peer, tot.at[z], tot.at[z]).wait_send()

        @pl.when(z < FED)
        def _():
            z_send_one(STA, peer, st.at[head_rows(peer), :], sti.at[z]).wait_send()

        @pl.when(peer < FED)
        def _():
            z_send_one(DST, peer, dso.at[peer], dsf.at[head_rows(z), :]).wait_send()

        z_send_one(DTT, peer, dto.at[peer], dti.at[z]).wait_send()
        for k in range(1, 3):

            @pl.when(bit(z, k))
            def _(k=k):
                z_send_one(DZK + k, peer, dz.at[k, head_rows(peer), :], dzi.at[k, z]).wait_send()

            @pl.when(bit(peer, k))
            def _(k=k):
                z_send_one(ZKK + k, peer, zko.at[k, peer], zkf.at[k, head_rows(z), :]).wait_send()


def hand_over(*refs):
    sources, targets, held, sem = refs[:5], refs[5:10], refs[10:15], refs[15]
    taken = [pltpu.make_async_copy(src, mid, sem.at[0, i]) for i, (src, mid) in enumerate(zip(sources, held))]
    given = [pltpu.make_async_copy(mid, dst, sem.at[1, i]) for i, (mid, dst) in enumerate(zip(held, targets))]
    for copy in taken:
        copy.start()
    for first, second in zip(taken, given):
        first.wait()
        second.start()
    for copy in given:
        copy.wait()


def body(inputs, b_proj, c_proj, decay_log, level_weight, out_grad, final_state_grad):
    def vmem(*shape, dtype=F32):
        return pltpu.VMEM(shape, dtype)

    scratch = [
        vmem(TOK, COLS, dtype=BF16),
        vmem(TOK, COLS, dtype=BF16),
        vmem(TOK, N, dtype=BF16),
        vmem(TOK, N, dtype=BF16),
        vmem(NB, HQ, BLK),
        vmem(NB, 6, HQ, BLK),
        vmem(HQ, HP, N),
        vmem(COLS, TOK),
        vmem(COLS, TOK),
        vmem(COLS, TOK, dtype=BF16),
        vmem(N, TOK, dtype=BF16),
        vmem(N, TOK, dtype=BF16),
        vmem(HQ, TOK),
        vmem(HQ, TOK),
        vmem(HQ, TOK),
        vmem(3, HQ, TOK),
        vmem(NB, HQ, TOK),
        vmem(3, 2, COLS, TOK, dtype=BF16),
        vmem(2, COLS, TOK, dtype=BF16),
        vmem(TOK, TOK),
        vmem(TOK, TOK),
        vmem(COLS, TOK),
        vmem(TOK, COLS, dtype=BF16),
        vmem(3, COLS, N),
        vmem(COLS, N),
        vmem(NZ, HQ, BLK),
        vmem(3, NZ, HP, N),
        vmem(NZ, HP, N),
        vmem(NZ, HP, N),
        vmem(3, NZ, HP, N),
        vmem(NZ, 8, N),
        vmem(COLS, N),
        vmem(3, COLS, N),
        vmem(NZ, 8, N),
        vmem(6, HQ, TOK),
        vmem(N, TOK),
        vmem(NB, BLK, N),
        vmem(NB, BLK, N),
        vmem(NB, BLK, N),
        vmem(NB, BLK, N),
        vmem(NB, 6, HQ, BLK),
        vmem(NB, HQ, BLK),
        vmem(HQ, TOK),
        vmem(HQ, N),
        vmem(COLS, N),
        vmem(COLS, N),
        vmem(HQ, N),
        vmem(2, BLK, N),
        pltpu.SemaphoreType.DMA((6, NB, NB)),
        pltpu.SemaphoreType.DMA((6, NB, NB)),
        pltpu.SemaphoreType.DMA((10, NZ)),
        pltpu.SemaphoreType.DMA((10, NZ)),
        pltpu.SemaphoreType.DMA((2, NB)),
        pltpu.SemaphoreType.DMA((2, NB)),
        pltpu.SemaphoreType.DMA((NB, NB)),
        pltpu.SemaphoreType.DMA((NB, NB)),
        pltpu.SemaphoreType.DMA((4, NB)),
        pltpu.SemaphoreType.DMA((4, NB)),
        pltpu.SemaphoreType.DMA((8, NB)),
    ]
    anywhere = pl.BlockSpec(memory_space=pl.ANY)
    made = (
        jax.ShapeDtypeStruct((BLK, HEADS * HP), BF16),
        jax.ShapeDtypeStruct((BLK, N), F32),
        jax.ShapeDtypeStruct((BLK, N), F32),
        jax.ShapeDtypeStruct((6, HEADS, BLK), F32),
        jax.ShapeDtypeStruct((HEADS, BLK), F32),
    )
    results = pl.pallas_call(
        kernel,
        out_shape=made,
        in_specs=[anywhere] * 7,
        out_specs=[anywhere] * 5,
        scratch_shapes=scratch,
        compiler_params=pltpu.CompilerParams(
            collective_id=0, has_side_effects=True, vmem_limit_bytes=56 * 2**20
        ),
    )(
        inputs[0],
        out_grad[0],
        b_proj[0],
        c_proj[0],
        decay_log[0].T,
        jnp.transpose(level_weight[0], (1, 2, 0)),
        jnp.transpose(final_state_grad[0], (0, 2, 1)),
    )
    up, db, dc, wg, dg = pl.pallas_call(
        hand_over,
        out_shape=made,
        in_specs=[anywhere] * 5,
        out_specs=[anywhere] * 5,
        scratch_shapes=[*(pltpu.VMEM(m.shape, m.dtype) for m in made), pltpu.SemaphoreType.DMA((2, 5))],
        compiler_params=pltpu.CompilerParams(vmem_limit_bytes=56 * 2**20),
    )(*results)
    return (up[None], db[None], dc[None], dg.T[None], jnp.transpose(wg, (2, 0, 1))[None])


def solution(mesh):
    rows = P("section", "seq", None)
    deep = P("section", "seq", None, None)
    return jax.shard_map(
        body,
        mesh=mesh,
        in_specs=(rows, rows, rows, rows, deep, rows, P("section", None, None, None)),
        out_specs=(rows, rows, rows, rows, deep),
        check_vma=False,
    )
```
